32 devices in a mesh: parts: 2 (over x), blk: 16 (over z, y, core).
Axes of the slice: x: 2, y: 2, z: 4, core: 2. Of those that a mesh axis runs over, the one named last changes fastest.
Arguments:
- right_side: float32 [5, 8192, 128], P(None, ('parts', 'blk')), parts along dimension 1, may hold values from -24 to 24
- off_diag: bfloat16 [4, 5, 5, 8192, 128], P(None, None, None, ('parts', 'blk')), parts along dimension 3, may hold values from -3 to 3
- diag_block: float32 [5, 5, 8192, 128], P(None, None, ('parts', 'blk')), parts along dimension 2, may hold values from -1.2 to 12, as said below
- block_of_device: int32 [16], replicated, may hold values from 0 to 4, as said below
- interface_pairs: int32 [16, 2], P('blk'), may hold values from -1 to 28, as said below
- strip_order: int32 [16, 2, 128], P('blk'), may hold values from 0 to 127, as said below
Outputs:
- update: float32 [5, 8192, 128], P(None, ('parts', 'blk')), parts along dimension 1
The draws below stay inside these ranges and needn't reach their ends.
There are 2 independent parts, one for each index of `parts`. The reference program is written for one: setup_inputs(seed, part) draws one part's arguments, and reference() takes and returns one part's arrays. A program takes and returns all parts, laid end to end along the dimension named above; an argument that names none is the same for every part. Nothing has to cross between parts.
Inputs may be any that keep to these rules, and one draw needn't show every extreme that they name: `block_of_device`: each of the 5 blocks is a nonempty run of consecutive devices on the cycle of devices; block 0 begins at device 16 - 2 and holds devices 16 - 2, 15 and 0, and the block numbers rise by one at each block start after device 0. `interface_pairs`: at the first device of a block (column 0) and at its last device (column 1) the entry is 2 p + t, naming the matched end: device p, its first-row side (t = 0) or last-row side (t = 1), which is itself the first or last device of a block. The matching pairs up all 10 block ends and is mutual. All other entries are -1. `strip_order`: each row is either 0, 1, ..., 127 or its reversal; the two sides of a matched pair use the same one; sides that are no block end hold 0, 1, ..., 127. `diag_block`: in every cell's 5x5 block, each diagonal entry exceeds the sum of the magnitudes of the other entries of its row.
All inputs are finite; a program needn't handle non-finite values.
Results may differ from the reference program's by a relative error of at most 0.0003.
Values sent between devices are 32-bit elements; how exact they have to be, the bound alone decides.
No kernel may reach another device: no remote copies, remote signals or barrier semaphores. Data moves between devices by JAX's collectives and lax.ppermute only.
A program may use at most 128 MiB of HBM per device.

```python
import jax
import jax.numpy as jnp

CI = 256
CJ = 128
BLOCKS = 5
SWEEPS = 2
NI = 4096
N_BLK = 16


def layout(key):
    folded = jax.random.fold_in(key, 11)
    key_cut, key_pair, key_flip = jax.random.split(folded, 3)
    scores = jax.random.permutation(key_cut, N_BLK - 3) + 1
    inner_cuts = jnp.sort(scores[:BLOCKS - 1]).astype(jnp.int32)
    cut_points = jnp.concatenate([inner_cuts, jnp.full((1,), N_BLK - 2, jnp.int32)]).astype(jnp.int32)
    devices = jnp.arange(N_BLK, dtype=jnp.int32)
    owners = (jnp.sum((devices[:, None] >= cut_points[None, :]).astype(jnp.int32), axis=1) % BLOCKS).astype(jnp.int32)
    first_dev = jnp.concatenate([cut_points[BLOCKS - 1:], cut_points[:BLOCKS - 1]])
    last_dev = cut_points - 1
    end_device = jnp.stack([first_dev, last_dev], axis=1).reshape(2 * BLOCKS)
    shuffled = jax.random.permutation(key_pair, 2 * BLOCKS).astype(jnp.int32)
    matched = jnp.zeros((2 * BLOCKS,), jnp.int32)
    matched = matched.at[shuffled[0::2]].set(shuffled[1::2]).at[shuffled[1::2]].set(shuffled[0::2])
    end_codes = end_device[matched] * 2 + matched % 2
    flip_bits = jax.random.randint(key_flip, (BLOCKS,), 0, 2).astype(jnp.int32)
    flip_end = jnp.zeros((2 * BLOCKS,), jnp.int32)
    flip_end = flip_end.at[shuffled[0::2]].set(flip_bits).at[shuffled[1::2]].set(flip_bits)
    end_side = jnp.arange(2 * BLOCKS, dtype=jnp.int32) % 2
    pair_codes = jnp.full((N_BLK, 2), -1, jnp.int32).at[end_device, end_side].set(end_codes)
    column = jnp.arange(CJ, dtype=jnp.int32)
    reversed_rows = jnp.where(flip_end[:, None] == 1, CJ - 1 - column[None, :], column[None, :])
    orders = jnp.broadcast_to(column, (N_BLK, 2, CJ)).astype(jnp.int32)
    orders = orders.at[end_device, end_side].set(reversed_rows)
    return (owners, pair_codes, orders)


def draw_block_of_device(key, part):
    return layout(key)[0]


def draw_interface_pairs(key, part):
    return layout(key)[1]


def draw_strip_order(key, part):
    return layout(key)[2]


def draw_diag_block(key, part):
    key_dom, key_off = jax.random.split(jax.random.fold_in(key, 23))
    dominant = 6.0 + 3.0 * jax.random.uniform(key_dom, (5, NI, CJ), jnp.float32)
    coupling = jnp.clip(0.5 * jax.random.normal(key_off, (5, 5, NI, CJ), jnp.float32), -1.2, 1.2)
    identity = jnp.eye(5, dtype=jnp.float32)[:, :, None, None]
    return identity * dominant[:, None] + (1.0 - identity) * coupling


def levels(stream_key, dims, shards, smallest, top_value):
    factor_of = 1.0
    for dim, shards_of in shards:
        draws = jax.random.uniform(jax.random.fold_in(jax.random.fold_in(stream_key, 6), dim), (shards_of,), jnp.float32, smallest / len(shards), top_value / len(shards))
        factor_of = factor_of * jnp.repeat(jnp.exp(draws), dims[dim] // shards_of).reshape((-1,) + (1,) * (len(dims) - 1 - dim))
    return factor_of


def centred(stream_key, dims, spread, limit, cuts=(), kind=jnp.bfloat16):
    array = jax.random.normal(stream_key, dims, jnp.float32) * spread
    if len(cuts) > 0:
        array = levels(stream_key, dims, cuts, -0.22, 0.18) * array
    return jnp.clip(array, min=-limit, max=limit).astype(kind)


def setup_inputs(seed: int = 0, part: int = 0) -> dict:
    arg_keys = jax.random.split(jax.random.key(seed), 7)
    own_keys = jax.random.split(jax.random.fold_in(arg_keys[6], part), 7)
    return {
        "right_side": centred(own_keys[0], (5, NI, CJ), 4.0, 24.0, ((1, 16),), jnp.float32),
        "off_diag": centred(own_keys[1], (4, 5, 5, NI, CJ), 0.6, 3.0, ((3, 16),)),
        "diag_block": draw_diag_block(jax.random.fold_in(jax.random.fold_in(arg_keys[6], part), 71), part),
        "block_of_device": draw_block_of_device(jax.random.fold_in(arg_keys[6], 71), part),
        "interface_pairs": draw_interface_pairs(jax.random.fold_in(arg_keys[6], 71), part),
        "strip_order": draw_strip_order(jax.random.fold_in(arg_keys[6], 71), part),
    }


def factor(diag_block):
    entries = [[diag_block[row_at, col_at] for col_at in range(5)] for row_at in range(5)]
    multipliers = {}
    for pivot_at in range(5):
        for row_at in range(pivot_at + 1, 5):
            scale_now = entries[row_at][pivot_at] / entries[pivot_at][pivot_at]
            multipliers[(row_at, pivot_at)] = scale_now
            for col_at in range(pivot_at + 1, 5):
                entries[row_at][col_at] = entries[row_at][col_at] - scale_now * entries[pivot_at][col_at]
    return multipliers, entries


def substitute(factors, vector):
    multipliers, upper_rows = factors
    forward = []
    for row_at in range(5):
        running = vector[row_at]
        for col_at in range(row_at):
            running = running - multipliers[(row_at, col_at)] * forward[col_at]
        forward.append(running)
    result = [None] * 5
    for row_at in reversed(range(5)):
        running = forward[row_at]
        for col_at in range(row_at + 1, 5):
            running = running - upper_rows[row_at][col_at] * result[col_at]
        result[row_at] = running / upper_rows[row_at][row_at]
    return jnp.stack(result)


def couple(off_diag, neighbours):
    coupled = jnp.zeros(neighbours[0].shape, jnp.float32)
    for face in range(4):
        for component in range(5):
            coupled = coupled + off_diag[face, :, component] * neighbours[face][component][None]
    return coupled


def reference(right_side, off_diag, diag_block, block_of_device, interface_pairs, strip_order):
    factors = factor(diag_block)
    update = substitute(factors, [right_side[component] for component in range(5)])
    devices = jnp.arange(N_BLK, dtype=jnp.int32)
    owners = block_of_device
    first_end = owners[(devices - 1) % N_BLK] != owners
    last_end = owners[(devices + 1) % N_BLK] != owners
    end_codes = jnp.maximum(interface_pairs, 0)
    partner = end_codes // 2
    partner_side = end_codes % 2
    for sweep_no in range(SWEEPS):
        grid = update.reshape(5, N_BLK, CI, CJ)
        low_rows = grid[:, :, 0]
        high_rows = grid[:, :, -1]
        edge_all = jnp.stack([low_rows, high_rows]).transpose(2, 0, 1, 3)
        incoming = edge_all[partner, partner_side]
        strips = jnp.take_along_axis(incoming, strip_order[:, :, None, :], axis=3)
        from_below = jnp.roll(high_rows, 1, axis=1)
        from_above = jnp.roll(low_rows, -1, axis=1)
        west_edge = jnp.where(first_end[None, :, None], strips[:, 0].transpose(1, 0, 2), from_below)
        east_edge = jnp.where(last_end[None, :, None], strips[:, 1].transpose(1, 0, 2), from_above)
        west_side = jnp.concatenate([west_edge[:, :, None], grid[:, :, :-1]], axis=2).reshape(5, NI, CJ)
        east_side = jnp.concatenate([grid[:, :, 1:], east_edge[:, :, None]], axis=2).reshape(5, NI, CJ)
        zero_column = jnp.zeros((5, NI, 1), jnp.float32)
        south_side = jnp.concatenate([zero_column, update[:, :, :-1]], axis=2)
        north_side = jnp.concatenate([update[:, :, 1:], zero_column], axis=2)
        coupled = couple(off_diag, [west_side, east_side, south_side, north_side])
        update = substitute(factors, [right_side[component] - coupled[component] for component in range(5)])
    return update
```

```python
import functools

import jax
import jax.numpy as jnp
from jax import lax
from jax.experimental import pallas as pl
from jax.experimental.pallas import tpu as pltpu
from jax.sharding import PartitionSpec as P

F32 = jnp.float32
VMEM = pltpu.VMEM
TOKEN = 40
A_AT, M_AT, CODE_AT = 5, 10, 35
PLANE = 4
MIB = 2**20


def lu(entries):
    entries = [list(row) for row in entries]
    for pivot_at in range(5):
        inverse = 1.0 / entries[pivot_at][pivot_at]
        for row_at in range(pivot_at + 1, 5):
            scale_now = entries[row_at][pivot_at] * inverse
            entries[row_at][pivot_at] = scale_now
            for col_at in range(pivot_at + 1, 5):
                entries[row_at][col_at] = (
                    entries[row_at][col_at] - scale_now * entries[pivot_at][col_at]
                )
        entries[pivot_at][pivot_at] = inverse
    return entries


def solve(factor_at, vector):
    forward = []
    for row_at in range(5):
        running = vector[row_at]
        for col_at in range(row_at):
            running = running - factor_at(row_at, col_at) * forward[col_at]
        forward.append(running)
    result = [None] * 5
    for row_at in reversed(range(5)):
        running = forward[row_at]
        for col_at in range(row_at + 1, 5):
            running = running - factor_at(row_at, col_at) * result[col_at]
        result[row_at] = running * factor_at(row_at, row_at)
    return result


def south(value, lane):
    return jnp.where(lane == 0, 0.0, pltpu.roll(value, 1, 1))


def north(value, lane):
    return jnp.where(lane == 127, 0.0, pltpu.roll(value, 127, 1))


def outer_face(side):
    return side


def edge_kernel(
    blocks, pairs, rhs_h, off_h, diag_h, token, factors, off_edge, rhs_edge, diag_edge, sems
):
    rows = rhs_h.shape[1]
    copies = []
    for side in range(2):
        at8, at16 = (0, 0) if side == 0 else (rows - 8, rows - 16)
        copies.append(
            (
                pltpu.make_async_copy(
                    diag_h.at[:, :, pl.ds(at8, 8)], diag_edge.at[side], sems.at[side, 0]
                ),
                pltpu.make_async_copy(
                    rhs_h.at[:, pl.ds(at8, 8)], rhs_edge.at[side], sems.at[side, 1]
                ),
                pltpu.make_async_copy(
                    off_h.at[:, :, :, pl.ds(at16, 16)], off_edge.at[side], sems.at[side, 2]
                ),
            )
        )
    for part in range(3):
        for side in range(2):
            copies[side][part].start()
    count = blocks.shape[0]
    me = lax.axis_index("blk")
    before = lax.rem(me + count - 1, count)
    after = lax.rem(me + 1, count)
    first_end = blocks[before] != blocks[me]
    last_end = blocks[after] != blocks[me]
    codes = (
        jnp.where(first_end, jnp.maximum(pairs[0, 0], 0), 2 * before + 1),
        jnp.where(last_end, jnp.maximum(pairs[0, 1], 0), 2 * after),
    )
    lane = lax.broadcasted_iota(jnp.int32, (8, 128), 1)
    for side in range(2):
        for part in range(3):
            copies[side][part].wait()
    for side in range(2):
        edge_row = 0 if side == 0 else 7
        half = slice(0, 8) if side == 0 else slice(8, 16)
        outer, inner = (0, 1) if side == 0 else (1, 0)

        def off(face, a, b):
            return off_edge[side, face, a, b].astype(F32)[half]

        e = lu([[diag_edge[side, a, b] for b in range(5)] for a in range(5)])
        for a in range(5):
            for b in range(5):
                factors[side, 5 * a + b] = e[a][b]
        factor_at = lambda a, b: e[a][b]
        rhs = [rhs_edge[side, a] for a in range(5)]
        u0 = solve(factor_at, rhs)
        acc = list(rhs)
        for b in range(5):
            around = (
                (inner, pltpu.roll(u0[b], 7 if side == 0 else 1, 0)),
                (2, south(u0[b], lane)),
                (3, north(u0[b], lane)),
            )
            for face, value in around:
                for a in range(5):
                    acc[a] = acc[a] - off(face, a, b) * value
        base = solve(factor_at, acc)
        at = TOKEN * side
        for a in range(5):
            token[pl.ds(at + a, 1)] = u0[a][edge_row : edge_row + 1]
            token[pl.ds(at + A_AT + a, 1)] = base[a][edge_row : edge_row + 1]
        for b in range(5):
            column = solve(factor_at, [off(outer, a, b) for a in range(5)])
            for a in range(5):
                token[pl.ds(at + M_AT + 5 * a + b, 1)] = column[a][edge_row : edge_row + 1]
        token[pl.ds(at + CODE_AT, 1)] = jnp.full((1, 128), codes[side], jnp.int32).astype(F32)
        token[pl.ds(at + CODE_AT + 1, TOKEN - CODE_AT - 1)] = jnp.zeros(
            (TOKEN - CODE_AT - 1, 128), F32
        )


def interior_kernel(rhs, off, diag, out_h, edges, factors, now, later, sems):
    rows = rhs.shape[1]
    tile1, tile2 = 32, 64
    for b in range(5):
        for field in (now, later):
            field[b, 0:8] = jnp.zeros((8, 128), F32)
            field[b, 8 + rows : 16 + rows] = jnp.zeros((8, 128), F32)

    def first(step, _):
        at = pl.multiple_of(step * tile1, tile1)
        here = pl.ds(at, tile1)
        e = lu([[diag[a, b, here] for b in range(5)] for a in range(5)])
        for a in range(5):
            for b in range(5):
                factors[a, b, here] = e[a][b]
        u0 = solve(lambda a, b: e[a][b], [rhs[a, here] for a in range(5)])
        for a in range(5):
            now[a, pl.ds(at + 8, tile1)] = u0[a]
        return 0

    lax.fori_loop(0, rows // tile1, first, 0)
    lane = lax.broadcasted_iota(jnp.int32, (tile2, 128), 1)
    for source, target in ((now, later), (later, now)):

        def sweep(step, _):
            at = pl.multiple_of(step * tile2, tile2)
            here = pl.ds(at, tile2)
            acc = [rhs[a, here] for a in range(5)]
            for b in range(5):
                middle = source[b, pl.ds(at + 8, tile2)]
                around = (
                    source[b, pl.ds(at + 7, tile2)],
                    source[b, pl.ds(at + 9, tile2)],
                    south(middle, lane),
                    north(middle, lane),
                )
                for face in range(4):
                    for a in range(5):
                        acc[a] = acc[a] - off[face, a, b, here].astype(F32) * around[face]
            fresh = solve(lambda a, b: factors[a, b, here], acc)
            for a in range(5):
                target[a, pl.ds(at + 8, tile2)] = fresh[a]
            return 0

        lax.fori_loop(0, rows // tile2, sweep, 0)
    copy = pltpu.make_async_copy(now.at[:, pl.ds(8, rows)], out_h, sems.at[0])
    copy.start()
    for a in range(5):
        edges[0, a] = now[a, 8:16]
        edges[1, a] = now[a, rows : rows + 8]
    copy.wait()


def select_kernel(*refs):
    lines = len(refs) - PLANE
    tokens, outs = refs[:lines], refs[lines:]
    me = lax.axis_index("blk")
    for other in range(PLANE):
        for slot in range(2):
            wanted = (2 * (me ^ other) + slot).astype(F32)
            found = jnp.zeros((TOKEN, 128), F32)
            for token in tokens:
                for side in range(2):
                    code = token[pl.ds(TOKEN * side + CODE_AT, 1)]
                    value = token[pl.ds(TOKEN * side, TOKEN)]
                    found = jnp.where(code == wanted, value, found)
            outs[other][pl.ds(TOKEN * slot, TOKEN)] = found


def finish_kernel(*refs):
    out_in, own, *arrived = refs[: 2 + PLANE]
    order, off_edge, factors, edges, out_h, beyond, result, sems = refs[2 + PLANE :]
    rows = out_h.shape[1]
    me = lax.axis_index("blk")
    lane = lax.broadcasted_iota(jnp.int32, (8, 128), 1)
    row = lax.broadcasted_iota(jnp.int32, (8, 128), 0)
    copies = []
    for side in range(2):
        at = TOKEN * side
        half = slice(0, 8) if side == 0 else slice(8, 16)
        edge_row, next_row = (0, 1) if side == 0 else (7, 6)
        outer = outer_face(side)
        source = own[pl.ds(at + CODE_AT, 1)].astype(jnp.int32) // 2
        found = arrived[0][pl.ds(at, TOKEN)]
        for other in range(1, PLANE):
            here = lax.rem(source, PLANE) == ((me ^ other) % PLANE)
            found = jnp.where(here, arrived[other][pl.ds(at, TOKEN)], found)
        columns = jnp.broadcast_to(order[0, side : side + 1], (TOKEN, 128))
        beyond[side] = jnp.take_along_axis(found, columns, axis=1)

        def mine(k):
            return own[pl.ds(at + k, 1)]

        def theirs(k):
            return beyond[side, pl.ds(k, 1)]

        def off(face, a, b):
            return off_edge[side, face, a, b].astype(F32)[half]

        acc = [jnp.zeros((8, 128), F32) for _ in range(5)]
        ahead, change = [], []
        for a in range(5):
            u1, delta = theirs(A_AT + a), jnp.zeros((1, 128), F32)
            for b in range(5):
                u1 = u1 - theirs(M_AT + 5 * a + b) * mine(b)
                delta = delta - mine(M_AT + 5 * a + b) * theirs(b)
            ahead.append(jnp.broadcast_to(u1, (8, 128)))
            change.append(jnp.broadcast_to(delta, (8, 128)))
        for b in range(5):
            at_edge = row == edge_row
            around = (
                (outer, jnp.where(at_edge, ahead[b], jnp.where(row == next_row, change[b], 0.0))),
                (2, jnp.where(at_edge, south(change[b], lane), 0.0)),
                (3, jnp.where(at_edge, north(change[b], lane), 0.0)),
            )
            for face, value in around:
                for a in range(5):
                    acc[a] = acc[a] + off(face, a, b) * value
        less = solve(lambda a, b: factors[side, 5 * a + b], acc)
        for a in range(5):
            result[side, a] = edges[side, a] - less[a]
        copies.append(
            pltpu.make_async_copy(
                result.at[side],
                out_h.at[:, pl.ds(0 if side == 0 else rows - 8, 8)],
                sems.at[side],
            )
        )
        copies[-1].start()
    for copy in copies:
        copy.wait()


def in_vmem(value):
    return pltpu.with_memory_space_constraint(value, VMEM)


def in_hbm(value):
    return pltpu.with_memory_space_constraint(value, pltpu.HBM)


def crossed(value, by):
    count = lax.axis_size("blk")
    return lax.ppermute(value, "blk", [(i, i ^ by) for i in range(count)])


def on_device(right_side, off_diag, diag_block, block_of_device, interface_pairs, strip_order):
    count = lax.axis_size("blk")
    rows = right_side.shape[1]
    any_space = pl.BlockSpec(memory_space=pl.ANY)
    in_smem = pl.BlockSpec(memory_space=pltpu.SMEM)
    whole = pl.BlockSpec(memory_space=VMEM)
    token, factors_edge, off_edge = pl.pallas_call(
        edge_kernel,
        out_shape=(
            VMEM((2 * TOKEN, 128), F32),
            VMEM((2, 25, 8, 128), F32),
            VMEM((2, 4, 5, 5, 16, 128), off_diag.dtype),
        ),
        in_specs=[in_smem, in_smem, any_space, any_space, any_space],
        out_specs=(whole, whole, whole),
        scratch_shapes=[
            VMEM((2, 5, 8, 128), F32),
            VMEM((2, 5, 5, 8, 128), F32),
            pltpu.SemaphoreType.DMA((2, 3)),
        ],
        compiler_params=pltpu.CompilerParams(vmem_limit_bytes=8 * MIB),
        name="edges",
    )(block_of_device, interface_pairs, in_hbm(right_side), in_hbm(off_diag), in_hbm(diag_block))

    lines = count // PLANE
    if lines <= 8:
        tokens = [token] + [crossed(token, PLANE * k) for k in range(1, lines)]
    else:
        groups = [[PLANE * k + j for k in range(lines)] for j in range(PLANE)]
        gathered = lax.all_gather(token, "blk", axis_index_groups=groups)
        tokens = [gathered[k] for k in range(lines)]

    inside, edges = pl.pallas_call(
        interior_kernel,
        out_shape=(pltpu.HBM(right_side.shape, F32), VMEM((2, 5, 8, 128), F32)),
        in_specs=[whole, whole, whole],
        out_specs=(any_space, whole),
        scratch_shapes=[
            VMEM((5, 5, rows, 128), F32),
            VMEM((5, rows + 16, 128), F32),
            VMEM((5, rows + 16, 128), F32),
            pltpu.SemaphoreType.DMA((1,)),
        ],
        compiler_params=pltpu.CompilerParams(vmem_limit_bytes=16 * MIB),
        cost_estimate=pl.CostEstimate(
            flops=32000000, bytes_accessed=12 * MIB, transcendentals=0
        ),
        name="interior",
    )(in_vmem(right_side), in_vmem(off_diag), in_vmem(diag_block))

    chosen = pl.pallas_call(
        select_kernel,
        out_shape=[VMEM((2 * TOKEN, 128), F32)] * PLANE,
        in_specs=[whole] * len(tokens),
        out_specs=[whole] * PLANE,
        compiler_params=pltpu.CompilerParams(vmem_limit_bytes=8 * MIB),
        name="choose",
    )(*[in_vmem(value) for value in tokens])
    arrived = [chosen[0]] + [crossed(chosen[k], k) for k in range(1, PLANE)]

    return pl.pallas_call(
        finish_kernel,
        out_shape=pltpu.HBM(right_side.shape, F32),
        in_specs=[any_space] + [whole] * (1 + PLANE + 4),
        out_specs=any_space,
        scratch_shapes=[
            VMEM((2, TOKEN, 128), F32),
            VMEM((2, 5, 8, 128), F32),
            pltpu.SemaphoreType.DMA((2,)),
        ],
        input_output_aliases={0: 0},
        compiler_params=pltpu.CompilerParams(vmem_limit_bytes=8 * MIB),
        name="finish",
    )(
        in_hbm(inside),
        in_vmem(token),
        *[in_vmem(value) for value in arrived],
        strip_order,
        in_vmem(off_edge),
        in_vmem(factors_edge),
        in_vmem(edges),
    )


def solution(mesh):
    return jax.shard_map(
        on_device,
        mesh=mesh,
        in_specs=(
            P(None, ("parts", "blk"), None),
            P(None, None, None, ("parts", "blk"), None),
            P(None, None, ("parts", "blk"), None),
            P(),
            P("blk", None),
            P("blk", None, None),
        ),
        out_specs=P(None, ("parts", "blk"), None),
        check_vma=False,
    )
```

```python
import functools

import jax
import jax.numpy as jnp
from jax import lax
from jax.experimental import pallas as pl
from jax.experimental.pallas import tpu as pltpu
from jax.sharding import PartitionSpec as P

F32 = jnp.float32
VMEM = pltpu.VMEM
TOKEN = 40
A_AT, M_AT, CODE_AT = 5, 10, 35
PLANE = 4
MIB = 2**20
FACTOR_TILE, TILE = 32, 64
LINE_ORDER = (2, 3, 1)
PLANE_ORDER = (3, 2, 1)


def lu(entries):
    entries = [list(row) for row in entries]
    for pivot_at in range(5):
        inverse = 1.0 / entries[pivot_at][pivot_at]
        for row_at in range(pivot_at + 1, 5):
            scale_now = entries[row_at][pivot_at] * inverse
            entries[row_at][pivot_at] = scale_now
            for col_at in range(pivot_at + 1, 5):
                entries[row_at][col_at] = (
                    entries[row_at][col_at] - scale_now * entries[pivot_at][col_at]
                )
        entries[pivot_at][pivot_at] = inverse
    return entries


def solve(factor_at, vector):
    forward = []
    for row_at in range(5):
        running = vector[row_at]
        for col_at in range(row_at):
            running = running - factor_at(row_at, col_at) * forward[col_at]
        forward.append(running)
    result = [None] * 5
    for row_at in reversed(range(5)):
        running = forward[row_at]
        for col_at in range(row_at + 1, 5):
            running = running - factor_at(row_at, col_at) * result[col_at]
        result[row_at] = running * factor_at(row_at, row_at)
    return result


def south(value, lane):
    return jnp.where(lane == 0, 0.0, pltpu.roll(value, 1, 1))


def north(value, lane):
    return jnp.where(lane == 127, 0.0, pltpu.roll(value, 127, 1))


def outer_face(side):
    return side


def edge_kernel(
    blocks_h,
    pairs_h,
    rhs_h,
    off_h,
    diag_h,
    token,
    factors,
    off_edge,
    blocks,
    pairs,
    rhs_edge,
    diag_edge,
    sems,
    scalar_sems,
):
    rows = rhs_h.shape[1]
    scalars = (
        pltpu.make_async_copy(blocks_h, blocks, scalar_sems.at[0]),
        pltpu.make_async_copy(pairs_h, pairs, scalar_sems.at[1]),
    )
    copies = []
    for side in range(2):
        at8, at16 = (0, 0) if side == 0 else (rows - 8, rows - 16)
        copies.append(
            (
                pltpu.make_async_copy(
                    diag_h.at[:, :, pl.ds(at8, 8)], diag_edge.at[side], sems.at[side, 0]
                ),
                pltpu.make_async_copy(
                    rhs_h.at[:, pl.ds(at8, 8)], rhs_edge.at[side], sems.at[side, 1]
                ),
                pltpu.make_async_copy(
                    off_h.at[:, :, :, pl.ds(at16, 16)], off_edge.at[side], sems.at[side, 2]
                ),
            )
        )
    for part in range(3):
        for side in range(2):
            copies[side][part].start()
    for copy in scalars:
        copy.start()
    for copy in scalars:
        copy.wait()
    count = blocks.shape[0]
    me = lax.axis_index("blk")
    before = lax.rem(me + count - 1, count)
    after = lax.rem(me + 1, count)
    first_end = blocks[before] != blocks[me]
    last_end = blocks[after] != blocks[me]
    codes = (
        jnp.where(first_end, jnp.maximum(pairs[0, 0], 0), 2 * before + 1),
        jnp.where(last_end, jnp.maximum(pairs[0, 1], 0), 2 * after),
    )
    lane = lax.broadcasted_iota(jnp.int32, (8, 128), 1)
    for side in range(2):
        for part in range(3):
            copies[side][part].wait()
    for side in range(2):
        edge_row = 0 if side == 0 else 7
        half = slice(0, 8) if side == 0 else slice(8, 16)
        outer, inner = (0, 1) if side == 0 else (1, 0)

        def off(face, a, b):
            return off_edge[side, face, a, b].astype(F32)[half]

        e = lu([[diag_edge[side, a, b] for b in range(5)] for a in range(5)])
        for a in range(5):
            for b in range(5):
                factors[side, 5 * a + b] = e[a][b]
        factor_at = lambda a, b: e[a][b]
        rhs = [rhs_edge[side, a] for a in range(5)]
        u0 = solve(factor_at, rhs)
        acc = list(rhs)
        for b in range(5):
            around = (
                (inner, pltpu.roll(u0[b], 7 if side == 0 else 1, 0)),
                (2, south(u0[b], lane)),
                (3, north(u0[b], lane)),
            )
            for face, value in around:
                for a in range(5):
                    acc[a] = acc[a] - off(face, a, b) * value
        base = solve(factor_at, acc)
        at = TOKEN * side
        for a in range(5):
            token[pl.ds(at + a, 1)] = u0[a][edge_row : edge_row + 1]
            token[pl.ds(at + A_AT + a, 1)] = base[a][edge_row : edge_row + 1]
        for b in range(5):
            column = solve(factor_at, [off(outer, a, b) for a in range(5)])
            for a in range(5):
                token[pl.ds(at + M_AT + 5 * a + b, 1)] = column[a][edge_row : edge_row + 1]
        token[pl.ds(at + CODE_AT, 1)] = jnp.full((1, 128), codes[side], jnp.int32).astype(F32)
        token[pl.ds(at + CODE_AT + 1, TOKEN - CODE_AT - 1)] = jnp.zeros(
            (TOKEN - CODE_AT - 1, 128), F32
        )


def sweep_rows(source, rhs, off, factors, at, tile):
    lane = lax.broadcasted_iota(jnp.int32, (tile, 128), 1)
    here = pl.ds(at, tile)
    acc = [rhs[a, here] for a in range(5)]
    for b in range(5):
        middle = source[b, pl.ds(at + 8, tile)]
        around = (
            source[b, pl.ds(at + 7, tile)],
            source[b, pl.ds(at + 9, tile)],
            south(middle, lane),
            north(middle, lane),
        )
        for face in range(4):
            for a in range(5):
                acc[a] = acc[a] - off[face, a, b, here].astype(F32) * around[face]
    return solve(lambda a, b: factors[a, b, here], acc)


def early_kernel(token, rhs, off, diag, factors, first_sweep, upper, start):
    del token
    rows = rhs.shape[1]
    for b in range(5):
        for field in (start, first_sweep):
            field[b, 0:8] = jnp.zeros((8, 128), F32)
            field[b, 8 + rows : 16 + rows] = jnp.zeros((8, 128), F32)

    def factor_step(step, _):
        at = pl.multiple_of(step * FACTOR_TILE, FACTOR_TILE)
        here = pl.ds(at, FACTOR_TILE)
        e = lu([[diag[a, b, here] for b in range(5)] for a in range(5)])
        for a in range(5):
            for b in range(5):
                factors[a, b, here] = e[a][b]
        u0 = solve(lambda a, b: e[a][b], [rhs[a, here] for a in range(5)])
        for a in range(5):
            start[a, pl.ds(at + 8, FACTOR_TILE)] = u0[a]
        return 0

    def first_step(step, _):
        at = pl.multiple_of(step * TILE, TILE)
        fresh = sweep_rows(start, rhs, off, factors, at, TILE)
        for a in range(5):
            first_sweep[a, pl.ds(at + 8, TILE)] = fresh[a]
        return 0

    def second_step(step, _):
        at = pl.multiple_of(step * TILE, TILE)
        fresh = sweep_rows(first_sweep, rhs, off, factors, at, TILE)
        for a in range(5):
            upper[a, pl.ds(at, TILE)] = fresh[a]
        return 0

    lax.fori_loop(0, rows // FACTOR_TILE, factor_step, 0)
    lax.fori_loop(0, rows // TILE, first_step, 0)
    lax.fori_loop(0, upper.shape[1] // TILE, second_step, 0)


def late_kernel(rhs, off, factors, first_sweep, upper, out_h, lower, sems):
    done, left = upper.shape[1], lower.shape[1]
    copies = (
        pltpu.make_async_copy(upper, out_h.at[:, pl.ds(0, done)], sems.at[0]),
        pltpu.make_async_copy(lower, out_h.at[:, pl.ds(done, left)], sems.at[1]),
    )
    copies[0].start()

    def second_step(step, _):
        at = pl.multiple_of(step * TILE, TILE)
        fresh = sweep_rows(first_sweep, rhs, off, factors, done + at, TILE)
        for a in range(5):
            lower[a, pl.ds(at, TILE)] = fresh[a]
        return 0

    lax.fori_loop(0, left // TILE, second_step, 0)
    copies[1].start()
    for copy in copies:
        copy.wait()


def select_kernel(*refs):
    lines = len(refs) - PLANE - 1
    tokens, outs = refs[:lines], refs[lines + 1 :]
    me = lax.axis_index("blk")
    for other in range(PLANE):
        for slot in range(2):
            wanted = (2 * (me ^ other) + slot).astype(F32)
            found = jnp.zeros((TOKEN, 128), F32)
            for token in tokens:
                for side in range(2):
                    code = token[pl.ds(TOKEN * side + CODE_AT, 1)]
                    value = token[pl.ds(TOKEN * side, TOKEN)]
                    found = jnp.where(code == wanted, value, found)
            outs[other][pl.ds(TOKEN * slot, TOKEN)] = found


def finish_kernel(*refs):
    out_in, own, *arrived = refs[: 2 + PLANE]
    order, off_edge, factors, upper, lower, out_h, beyond, result, sems = refs[2 + PLANE :]
    rows = out_h.shape[1]
    me = lax.axis_index("blk")
    lane = lax.broadcasted_iota(jnp.int32, (8, 128), 1)
    row = lax.broadcasted_iota(jnp.int32, (8, 128), 0)
    copies = []
    for side in range(2):
        at = TOKEN * side
        half = slice(0, 8) if side == 0 else slice(8, 16)
        edge_row, next_row = (0, 1) if side == 0 else (7, 6)
        outer = outer_face(side)
        source = own[pl.ds(at + CODE_AT, 1)].astype(jnp.int32) // 2
        found = arrived[0][pl.ds(at, TOKEN)]
        for value, other in zip(arrived[1:], PLANE_ORDER):
            here = lax.rem(source, PLANE) == ((me ^ other) % PLANE)
            found = jnp.where(here, value[pl.ds(at, TOKEN)], found)
        columns = jnp.broadcast_to(order[0, side : side + 1], (TOKEN, 128))
        beyond[side] = jnp.take_along_axis(found, columns, axis=1)

        def mine(k):
            return own[pl.ds(at + k, 1)]

        def theirs(k):
            return beyond[side, pl.ds(k, 1)]

        def off(face, a, b):
            return off_edge[side, face, a, b].astype(F32)[half]

        acc = [jnp.zeros((8, 128), F32) for _ in range(5)]
        ahead, change = [], []
        for a in range(5):
            u1, delta = theirs(A_AT + a), jnp.zeros((1, 128), F32)
            for b in range(5):
                u1 = u1 - theirs(M_AT + 5 * a + b) * mine(b)
                delta = delta - mine(M_AT + 5 * a + b) * theirs(b)
            ahead.append(jnp.broadcast_to(u1, (8, 128)))
            change.append(jnp.broadcast_to(delta, (8, 128)))
        for b in range(5):
            at_edge = row == edge_row
            around = (
                (outer, jnp.where(at_edge, ahead[b], jnp.where(row == next_row, change[b], 0.0))),
                (2, jnp.where(at_edge, south(change[b], lane), 0.0)),
                (3, jnp.where(at_edge, north(change[b], lane), 0.0)),
            )
            for face, value in around:
                for a in range(5):
                    acc[a] = acc[a] + off(face, a, b) * value
        less = solve(lambda a, b: factors[side, 5 * a + b], acc)
        for a in range(5):
            near = upper[a, 0:8] if side == 0 else lower[a, pl.ds(lower.shape[1] - 8, 8)]
            result[side, a] = near - less[a]
        copies.append(
            pltpu.make_async_copy(
                result.at[side],
                out_h.at[:, pl.ds(0 if side == 0 else rows - 8, 8)],
                sems.at[side],
            )
        )
        copies[-1].start()
    for copy in copies:
        copy.wait()


def in_vmem(value):
    return pltpu.with_memory_space_constraint(value, VMEM)


def in_hbm(value):
    return pltpu.with_memory_space_constraint(value, pltpu.HBM)


def crossed(value, by):
    count = lax.axis_size("blk")
    return lax.ppermute(value, "blk", [(i, i ^ by) for i in range(count)])


def on_device(right_side, off_diag, diag_block, block_of_device, interface_pairs, strip_order):
    count = lax.axis_size("blk")
    rows = right_side.shape[1]
    any_space = pl.BlockSpec(memory_space=pl.ANY)
    whole = pl.BlockSpec(memory_space=VMEM)
    token, factors_edge, off_edge = pl.pallas_call(
        edge_kernel,
        out_shape=(
            VMEM((2 * TOKEN, 128), F32),
            VMEM((2, 25, 8, 128), F32),
            VMEM((2, 4, 5, 5, 16, 128), off_diag.dtype),
        ),
        in_specs=[any_space] * 5,
        out_specs=(whole, whole, whole),
        scratch_shapes=[
            pltpu.SMEM(block_of_device.shape, jnp.int32),
            pltpu.SMEM(interface_pairs.shape, jnp.int32),
            VMEM((2, 5, 8, 128), F32),
            VMEM((2, 5, 5, 8, 128), F32),
            pltpu.SemaphoreType.DMA((2, 3)),
            pltpu.SemaphoreType.DMA((2,)),
        ],
        compiler_params=pltpu.CompilerParams(vmem_limit_bytes=8 * MIB),
        name="edges",
    )(
        in_hbm(block_of_device),
        in_hbm(interface_pairs),
        in_hbm(right_side),
        in_hbm(off_diag),
        in_hbm(diag_block),
    )

    lines = count // PLANE
    if lines <= 8:
        order = LINE_ORDER if lines == 4 else range(1, lines)
        tokens = [token] + [crossed(token, PLANE * k) for k in order]
    else:
        groups = [[PLANE * k + j for k in range(lines)] for j in range(PLANE)]
        gathered = lax.all_gather(token, "blk", axis_index_groups=groups)
        tokens = [gathered[k] for k in range(lines)]

    rows_early = rows // 2 // TILE * TILE
    factors, first_sweep, upper = pl.pallas_call(
        early_kernel,
        out_shape=(
            VMEM((5, 5, rows, 128), F32),
            VMEM((5, rows + 16, 128), F32),
            VMEM((5, rows_early, 128), F32),
        ),
        in_specs=[any_space, whole, whole, whole],
        out_specs=(whole, whole, whole),
        scratch_shapes=[VMEM((5, rows + 16, 128), F32)],
        compiler_params=pltpu.CompilerParams(vmem_limit_bytes=12 * MIB),
        cost_estimate=pl.CostEstimate(
            flops=20000000, bytes_accessed=12 * MIB, transcendentals=0
        ),
        name="early",
    )(token, in_vmem(right_side), in_vmem(off_diag), in_vmem(diag_block))

    chosen = pl.pallas_call(
        select_kernel,
        out_shape=[VMEM((2 * TOKEN, 128), F32)] * PLANE,
        in_specs=[whole] * len(tokens) + [any_space],
        out_specs=[whole] * PLANE,
        compiler_params=pltpu.CompilerParams(vmem_limit_bytes=8 * MIB),
        name="choose",
    )(*[in_vmem(value) for value in tokens], upper)

    inside, lower = pl.pallas_call(
        late_kernel,
        out_shape=(
            pltpu.HBM(right_side.shape, F32),
            VMEM((5, rows - rows_early, 128), F32),
        ),
        in_specs=[whole] * 5,
        out_specs=(any_space, whole),
        scratch_shapes=[pltpu.SemaphoreType.DMA((2,))],
        compiler_params=pltpu.CompilerParams(vmem_limit_bytes=8 * MIB),
        cost_estimate=pl.CostEstimate(
            flops=8000000, bytes_accessed=6 * MIB, transcendentals=0
        ),
        name="late",
    )(*[in_vmem(value) for value in (right_side, off_diag, factors, first_sweep, upper)])
    arrived = [chosen[0]] + [crossed(chosen[k], k) for k in PLANE_ORDER]

    return pl.pallas_call(
        finish_kernel,
        out_shape=pltpu.HBM(right_side.shape, F32),
        in_specs=[any_space] + [whole] * (1 + PLANE + 5),
        out_specs=any_space,
        scratch_shapes=[
            VMEM((2, TOKEN, 128), F32),
            VMEM((2, 5, 8, 128), F32),
            pltpu.SemaphoreType.DMA((2,)),
        ],
        input_output_aliases={0: 0},
        compiler_params=pltpu.CompilerParams(vmem_limit_bytes=8 * MIB),
        name="finish",
    )(
        in_hbm(inside),
        in_vmem(token),
        *[in_vmem(value) for value in arrived],
        strip_order,
        in_vmem(off_edge),
        in_vmem(factors_edge),
        in_vmem(upper),
        in_vmem(lower),
    )


def solution(mesh):
    return jax.shard_map(
        on_device,
        mesh=mesh,
        in_specs=(
            P(None, ("parts", "blk"), None),
            P(None, None, None, ("parts", "blk"), None),
            P(None, None, ("parts", "blk"), None),
            P(),
            P("blk", None),
            P("blk", None, None),
        ),
        out_specs=P(None, ("parts", "blk"), None),
        check_vma=False,
    )
```

```python
import functools

import jax
import jax.numpy as jnp
from jax import lax
from jax.experimental import pallas as pl
from jax.experimental.pallas import tpu as pltpu
from jax.sharding import PartitionSpec as P

F32 = jnp.float32
VMEM = pltpu.VMEM
TOKEN = 40
A_AT, M_AT, CODE_AT = 5, 10, 35
PLANE = 4
MIB = 2**20
FACTOR_TILE, TILE = 32, 64
LINE_STEPS = ((2, 3, 1, 0), (3, 2, 0, 1), (1, 0, 3, 2))
PLANE_STEPS = ((3, 2, 1, 0), (2, 3, 0, 1), (1, 0, 3, 2))


def lu(entries):
    entries = [list(row) for row in entries]
    for pivot_at in range(5):
        inverse = 1.0 / entries[pivot_at][pivot_at]
        for row_at in range(pivot_at + 1, 5):
            scale_now = entries[row_at][pivot_at] * inverse
            entries[row_at][pivot_at] = scale_now
            for col_at in range(pivot_at + 1, 5):
                entries[row_at][col_at] = (
                    entries[row_at][col_at] - scale_now * entries[pivot_at][col_at]
                )
        entries[pivot_at][pivot_at] = inverse
    return entries


def solve(factor_at, vector):
    forward = []
    for row_at in range(5):
        running = vector[row_at]
        for col_at in range(row_at):
            running = running - factor_at(row_at, col_at) * forward[col_at]
        forward.append(running)
    result = [None] * 5
    for row_at in reversed(range(5)):
        running = forward[row_at]
        for col_at in range(row_at + 1, 5):
            running = running - factor_at(row_at, col_at) * result[col_at]
        result[row_at] = running * factor_at(row_at, row_at)
    return result


def south(value, lane):
    return jnp.where(lane == 0, 0.0, pltpu.roll(value, 1, 1))


def north(value, lane):
    return jnp.where(lane == 127, 0.0, pltpu.roll(value, 127, 1))


def outer_face(side):
    return side


def edge_kernel(
    blocks_h,
    pairs_h,
    rhs_h,
    off_h,
    diag_h,
    token,
    factors,
    off_edge,
    blocks,
    pairs,
    rhs_edge,
    diag_edge,
    sems,
    scalar_sems,
):
    rows = rhs_h.shape[1]
    scalars = (
        pltpu.make_async_copy(blocks_h, blocks, scalar_sems.at[0]),
        pltpu.make_async_copy(pairs_h, pairs, scalar_sems.at[1]),
    )
    copies = []
    for side in range(2):
        at8, at16 = (0, 0) if side == 0 else (rows - 8, rows - 16)
        copies.append(
            (
                pltpu.make_async_copy(
                    diag_h.at[:, :, pl.ds(at8, 8)], diag_edge.at[side], sems.at[side, 0]
                ),
                pltpu.make_async_copy(
                    rhs_h.at[:, pl.ds(at8, 8)], rhs_edge.at[side], sems.at[side, 1]
                ),
                pltpu.make_async_copy(
                    off_h.at[:, :, :, pl.ds(at16, 16)], off_edge.at[side], sems.at[side, 2]
                ),
            )
        )
    for part in range(3):
        for side in range(2):
            copies[side][part].start()
    for copy in scalars:
        copy.start()
    for copy in scalars:
        copy.wait()
    count = blocks.shape[0]
    me = lax.axis_index("blk")
    before = lax.rem(me + count - 1, count)
    after = lax.rem(me + 1, count)
    first_end = blocks[before] != blocks[me]
    last_end = blocks[after] != blocks[me]
    codes = (
        jnp.where(first_end, jnp.maximum(pairs[0, 0], 0), 2 * before + 1),
        jnp.where(last_end, jnp.maximum(pairs[0, 1], 0), 2 * after),
    )
    lane = lax.broadcasted_iota(jnp.int32, (8, 128), 1)
    for side in range(2):
        for part in range(3):
            copies[side][part].wait()
    for side in range(2):
        edge_row = 0 if side == 0 else 7
        half = slice(0, 8) if side == 0 else slice(8, 16)
        outer, inner = (0, 1) if side == 0 else (1, 0)

        def off(face, a, b):
            return off_edge[side, face, a, b].astype(F32)[half]

        e = lu([[diag_edge[side, a, b] for b in range(5)] for a in range(5)])
        for a in range(5):
            for b in range(5):
                factors[side, 5 * a + b] = e[a][b]
        factor_at = lambda a, b: e[a][b]
        rhs = [rhs_edge[side, a] for a in range(5)]
        u0 = solve(factor_at, rhs)
        acc = list(rhs)
        for b in range(5):
            around = (
                (inner, pltpu.roll(u0[b], 7 if side == 0 else 1, 0)),
                (2, south(u0[b], lane)),
                (3, north(u0[b], lane)),
            )
            for face, value in around:
                for a in range(5):
                    acc[a] = acc[a] - off(face, a, b) * value
        base = solve(factor_at, acc)
        at = TOKEN * side
        for a in range(5):
            token[pl.ds(at + a, 1)] = u0[a][edge_row : edge_row + 1]
            token[pl.ds(at + A_AT + a, 1)] = base[a][edge_row : edge_row + 1]
        for b in range(5):
            column = solve(factor_at, [off(outer, a, b) for a in range(5)])
            for a in range(5):
                token[pl.ds(at + M_AT + 5 * a + b, 1)] = column[a][edge_row : edge_row + 1]
        token[pl.ds(at + CODE_AT, 1)] = jnp.full((1, 128), codes[side], jnp.int32).astype(F32)
        token[pl.ds(at + CODE_AT + 1, TOKEN - CODE_AT - 1)] = jnp.zeros(
            (TOKEN - CODE_AT - 1, 128), F32
        )


def sweep_rows(source, rhs, off, factors, at, tile):
    lane = lax.broadcasted_iota(jnp.int32, (tile, 128), 1)
    here = pl.ds(at, tile)
    acc = [rhs[a, here] for a in range(5)]
    for b in range(5):
        middle = source[b, pl.ds(at + 8, tile)]
        around = (
            source[b, pl.ds(at + 7, tile)],
            source[b, pl.ds(at + 9, tile)],
            south(middle, lane),
            north(middle, lane),
        )
        for face in range(4):
            for a in range(5):
                acc[a] = acc[a] - off[face, a, b, here].astype(F32) * around[face]
    return solve(lambda a, b: factors[a, b, here], acc)


def early_kernel(token, rhs, off, diag, factors, first_sweep, upper, start):
    del token
    rows = rhs.shape[1]
    for b in range(5):
        for field in (start, first_sweep):
            field[b, 0:8] = jnp.zeros((8, 128), F32)
            field[b, 8 + rows : 16 + rows] = jnp.zeros((8, 128), F32)

    def factor_step(step, _):
        at = pl.multiple_of(step * FACTOR_TILE, FACTOR_TILE)
        here = pl.ds(at, FACTOR_TILE)
        e = lu([[diag[a, b, here] for b in range(5)] for a in range(5)])
        for a in range(5):
            for b in range(5):
                factors[a, b, here] = e[a][b]
        u0 = solve(lambda a, b: e[a][b], [rhs[a, here] for a in range(5)])
        for a in range(5):
            start[a, pl.ds(at + 8, FACTOR_TILE)] = u0[a]
        return 0

    def first_step(step, _):
        at = pl.multiple_of(step * TILE, TILE)
        fresh = sweep_rows(start, rhs, off, factors, at, TILE)
        for a in range(5):
            first_sweep[a, pl.ds(at + 8, TILE)] = fresh[a]
        return 0

    def second_step(step, _):
        at = pl.multiple_of(step * TILE, TILE)
        fresh = sweep_rows(first_sweep, rhs, off, factors, at, TILE)
        for a in range(5):
            upper[a, pl.ds(at, TILE)] = fresh[a]
        return 0

    lax.fori_loop(0, rows // FACTOR_TILE, factor_step, 0)
    lax.fori_loop(0, rows // TILE, first_step, 0)
    lax.fori_loop(0, upper.shape[1] // TILE, second_step, 0)


def late_kernel(rhs, off, factors, first_sweep, upper, out_h, lower, sems):
    done, left = upper.shape[1], lower.shape[1]
    copies = (
        pltpu.make_async_copy(upper, out_h.at[:, pl.ds(0, done)], sems.at[0]),
        pltpu.make_async_copy(lower, out_h.at[:, pl.ds(done, left)], sems.at[1]),
    )
    copies[0].start()

    def second_step(step, _):
        at = pl.multiple_of(step * TILE, TILE)
        fresh = sweep_rows(first_sweep, rhs, off, factors, done + at, TILE)
        for a in range(5):
            lower[a, pl.ds(at, TILE)] = fresh[a]
        return 0

    lax.fori_loop(0, left // TILE, second_step, 0)
    copies[1].start()
    for copy in copies:
        copy.wait()


def table(values, at):
    result = values[0]
    for k in range(1, len(values)):
        result = jnp.where(at == k, values[k], result)
    return result


def select_kernel(*refs):
    lines = len(refs) - PLANE - 1
    tokens, outs = refs[:lines], refs[lines + 1 :]
    me = lax.axis_index("blk")
    place = me % PLANE
    for out, step in zip(outs, (tuple(range(PLANE)),) + PLANE_STEPS):
        target = me - place + table(step, place)
        for slot in range(2):
            wanted = (2 * target + slot).astype(F32)
            found = jnp.zeros((TOKEN, 128), F32)
            for token in tokens:
                for side in range(2):
                    code = token[pl.ds(TOKEN * side + CODE_AT, 1)]
                    value = token[pl.ds(TOKEN * side, TOKEN)]
                    found = jnp.where(code == wanted, value, found)
            out[pl.ds(TOKEN * slot, TOKEN)] = found


def finish_kernel(*refs):
    out_in, own, *arrived = refs[: 2 + PLANE]
    order, off_edge, factors, upper, lower, out_h, beyond, result, sems = refs[2 + PLANE :]
    rows = out_h.shape[1]
    me = lax.axis_index("blk")
    lane = lax.broadcasted_iota(jnp.int32, (8, 128), 1)
    row = lax.broadcasted_iota(jnp.int32, (8, 128), 0)
    copies = []
    for side in range(2):
        at = TOKEN * side
        half = slice(0, 8) if side == 0 else slice(8, 16)
        edge_row, next_row = (0, 1) if side == 0 else (7, 6)
        outer = outer_face(side)
        source = own[pl.ds(at + CODE_AT, 1)].astype(jnp.int32) // 2
        found = arrived[0][pl.ds(at, TOKEN)]
        for value, step in zip(arrived[1:], PLANE_STEPS):
            sender = table([step.index(k) for k in range(PLANE)], me % PLANE)
            here = lax.rem(source, PLANE) == sender
            found = jnp.where(here, value[pl.ds(at, TOKEN)], found)
        columns = jnp.broadcast_to(order[0, side : side + 1], (TOKEN, 128))
        beyond[side] = jnp.take_along_axis(found, columns, axis=1)

        def mine(k):
            return own[pl.ds(at + k, 1)]

        def theirs(k):
            return beyond[side, pl.ds(k, 1)]

        def off(face, a, b):
            return off_edge[side, face, a, b].astype(F32)[half]

        acc = [jnp.zeros((8, 128), F32) for _ in range(5)]
        ahead, change = [], []
        for a in range(5):
            u1, delta = theirs(A_AT + a), jnp.zeros((1, 128), F32)
            for b in range(5):
                u1 = u1 - theirs(M_AT + 5 * a + b) * mine(b)
                delta = delta - mine(M_AT + 5 * a + b) * theirs(b)
            ahead.append(jnp.broadcast_to(u1, (8, 128)))
            change.append(jnp.broadcast_to(delta, (8, 128)))
        for b in range(5):
            at_edge = row == edge_row
            around = (
                (outer, jnp.where(at_edge, ahead[b], jnp.where(row == next_row, change[b], 0.0))),
                (2, jnp.where(at_edge, south(change[b], lane), 0.0)),
                (3, jnp.where(at_edge, north(change[b], lane), 0.0)),
            )
            for face, value in around:
                for a in range(5):
                    acc[a] = acc[a] + off(face, a, b) * value
        less = solve(lambda a, b: factors[side, 5 * a + b], acc)
        for a in range(5):
            near = upper[a, 0:8] if side == 0 else lower[a, pl.ds(lower.shape[1] - 8, 8)]
            result[side, a] = near - less[a]
        copies.append(
            pltpu.make_async_copy(
                result.at[side],
                out_h.at[:, pl.ds(0 if side == 0 else rows - 8, 8)],
                sems.at[side],
            )
        )
        copies[-1].start()
    for copy in copies:
        copy.wait()


def in_vmem(value):
    return pltpu.with_memory_space_constraint(value, VMEM)


def in_hbm(value):
    return pltpu.with_memory_space_constraint(value, pltpu.HBM)


def along_line(value, step):
    pairs = [(PLANE * k + j, PLANE * to + j) for k, to in enumerate(step) for j in range(PLANE)]
    return lax.ppermute(value, "blk", pairs)


def within_plane(value, step):
    lines = lax.axis_size("blk") // PLANE
    pairs = [(PLANE * k + j, PLANE * k + to) for k in range(lines) for j, to in enumerate(step)]
    return lax.ppermute(value, "blk", pairs)


def on_device(right_side, off_diag, diag_block, block_of_device, interface_pairs, strip_order):
    count = lax.axis_size("blk")
    rows = right_side.shape[1]
    any_space = pl.BlockSpec(memory_space=pl.ANY)
    whole = pl.BlockSpec(memory_space=VMEM)
    token, factors_edge, off_edge = pl.pallas_call(
        edge_kernel,
        out_shape=(
            VMEM((2 * TOKEN, 128), F32),
            VMEM((2, 25, 8, 128), F32),
            VMEM((2, 4, 5, 5, 16, 128), off_diag.dtype),
        ),
        in_specs=[any_space] * 5,
        out_specs=(whole, whole, whole),
        scratch_shapes=[
            pltpu.SMEM(block_of_device.shape, jnp.int32),
            pltpu.SMEM(interface_pairs.shape, jnp.int32),
            VMEM((2, 5, 8, 128), F32),
            VMEM((2, 5, 5, 8, 128), F32),
            pltpu.SemaphoreType.DMA((2, 3)),
            pltpu.SemaphoreType.DMA((2,)),
        ],
        compiler_params=pltpu.CompilerParams(vmem_limit_bytes=8 * MIB),
        name="edges",
    )(
        in_hbm(block_of_device),
        in_hbm(interface_pairs),
        in_hbm(right_side),
        in_hbm(off_diag),
        in_hbm(diag_block),
    )

    lines = count // PLANE
    if lines <= 8:
        steps = [[k ^ by for k in range(lines)] for by in range(1, lines)]
        if lines == len(LINE_STEPS[0]):
            steps = LINE_STEPS
        tokens = [token] + [along_line(token, step) for step in steps]
    else:
        groups = [[PLANE * k + j for k in range(lines)] for j in range(PLANE)]
        gathered = lax.all_gather(token, "blk", axis_index_groups=groups)
        tokens = [gathered[k] for k in range(lines)]

    rows_early = rows // 4 // TILE * TILE
    factors, first_sweep, upper = pl.pallas_call(
        early_kernel,
        out_shape=(
            VMEM((5, 5, rows, 128), F32),
            VMEM((5, rows + 16, 128), F32),
            VMEM((5, rows_early, 128), F32),
        ),
        in_specs=[any_space, whole, whole, whole],
        out_specs=(whole, whole, whole),
        scratch_shapes=[VMEM((5, rows + 16, 128), F32)],
        compiler_params=pltpu.CompilerParams(vmem_limit_bytes=12 * MIB),
        cost_estimate=pl.CostEstimate(
            flops=20000000, bytes_accessed=12 * MIB, transcendentals=0
        ),
        name="early",
    )(token, in_vmem(right_side), in_vmem(off_diag), in_vmem(diag_block))

    chosen = pl.pallas_call(
        select_kernel,
        out_shape=[VMEM((2 * TOKEN, 128), F32)] * PLANE,
        in_specs=[whole] * len(tokens) + [any_space],
        out_specs=[whole] * PLANE,
        compiler_params=pltpu.CompilerParams(vmem_limit_bytes=8 * MIB),
        name="choose",
    )(*[in_vmem(value) for value in tokens], upper)

    inside, lower = pl.pallas_call(
        late_kernel,
        out_shape=(
            pltpu.HBM(right_side.shape, F32),
            VMEM((5, rows - rows_early, 128), F32),
        ),
        in_specs=[whole] * 5,
        out_specs=(any_space, whole),
        scratch_shapes=[pltpu.SemaphoreType.DMA((2,))],
        compiler_params=pltpu.CompilerParams(vmem_limit_bytes=8 * MIB),
        cost_estimate=pl.CostEstimate(
            flops=8000000, bytes_accessed=6 * MIB, transcendentals=0
        ),
        name="late",
    )(*[in_vmem(value) for value in (right_side, off_diag, factors, first_sweep, upper)])
    arrived = [chosen[0]]
    for value, step in zip(chosen[1:], PLANE_STEPS):
        arrived.append(within_plane(value, step))

    return pl.pallas_call(
        finish_kernel,
        out_shape=pltpu.HBM(right_side.shape, F32),
        in_specs=[any_space] + [whole] * (1 + PLANE + 5),
        out_specs=any_space,
        scratch_shapes=[
            VMEM((2, TOKEN, 128), F32),
            VMEM((2, 5, 8, 128), F32),
            pltpu.SemaphoreType.DMA((2,)),
        ],
        input_output_aliases={0: 0},
        compiler_params=pltpu.CompilerParams(vmem_limit_bytes=8 * MIB),
        name="finish",
    )(
        in_hbm(inside),
        in_vmem(token),
        *[in_vmem(value) for value in arrived],
        strip_order,
        in_vmem(off_edge),
        in_vmem(factors_edge),
        in_vmem(upper),
        in_vmem(lower),
    )


def solution(mesh):
    return jax.shard_map(
        on_device,
        mesh=mesh,
        in_specs=(
            P(None, ("parts", "blk"), None),
            P(None, None, None, ("parts", "blk"), None),
            P(None, None, ("parts", "blk"), None),
            P(),
            P("blk", None),
            P("blk", None, None),
        ),
        out_specs=P(None, ("parts", "blk"), None),
        check_vma=False,
    )
```

```python
import functools

import jax
import jax.numpy as jnp
from jax import lax
from jax.experimental import pallas as pl
from jax.experimental.pallas import tpu as pltpu
from jax.sharding import PartitionSpec as P

F32 = jnp.float32
VMEM = pltpu.VMEM
TOKEN = 36
A_AT, M_AT, CODE_AT = 5, 10, 35
PLANE = 4
MIB = 2**20
FACTOR_TILE, TILE = 32, 64
LINE_STEPS = ((2, 3, 1, 0), (3, 2, 0, 1), (1, 0, 3, 2))
PLANE_STEPS = ((3, 2, 1, 0), (2, 3, 0, 1), (1, 0, 3, 2))


def lu(entries):
    entries = [list(row) for row in entries]
    for pivot_at in range(5):
        inverse = 1.0 / entries[pivot_at][pivot_at]
        for row_at in range(pivot_at + 1, 5):
            scale_now = entries[row_at][pivot_at] * inverse
            entries[row_at][pivot_at] = scale_now
            for col_at in range(pivot_at + 1, 5):
                entries[row_at][col_at] = (
                    entries[row_at][col_at] - scale_now * entries[pivot_at][col_at]
                )
        entries[pivot_at][pivot_at] = inverse
    return entries


def solve(factor_at, vector):
    forward = []
    for row_at in range(5):
        running = vector[row_at]
        for col_at in range(row_at):
            running = running - factor_at(row_at, col_at) * forward[col_at]
        forward.append(running)
    result = [None] * 5
    for row_at in reversed(range(5)):
        running = forward[row_at]
        for col_at in range(row_at + 1, 5):
            running = running - factor_at(row_at, col_at) * result[col_at]
        result[row_at] = running * factor_at(row_at, row_at)
    return result


def south(value, lane):
    return jnp.where(lane == 0, 0.0, pltpu.roll(value, 1, 1))


def north(value, lane):
    return jnp.where(lane == 127, 0.0, pltpu.roll(value, 127, 1))


def outer_face(side):
    return side


def edge_kernel(
    blocks_h,
    pairs_h,
    rhs_h,
    off_h,
    diag_h,
    token,
    factors,
    off_edge,
    blocks,
    pairs,
    rhs_edge,
    diag_edge,
    sems,
    scalar_sems,
):
    rows = rhs_h.shape[1]
    scalars = (
        pltpu.make_async_copy(blocks_h, blocks, scalar_sems.at[0]),
        pltpu.make_async_copy(pairs_h, pairs, scalar_sems.at[1]),
    )
    copies = []
    for side in range(2):
        at8, at16 = (0, 0) if side == 0 else (rows - 8, rows - 16)
        copies.append(
            (
                pltpu.make_async_copy(
                    diag_h.at[:, :, pl.ds(at8, 8)], diag_edge.at[side], sems.at[side, 0]
                ),
                pltpu.make_async_copy(
                    rhs_h.at[:, pl.ds(at8, 8)], rhs_edge.at[side], sems.at[side, 1]
                ),
                pltpu.make_async_copy(
                    off_h.at[:, :, :, pl.ds(at16, 16)], off_edge.at[side], sems.at[side, 2]
                ),
            )
        )
    for part in range(3):
        for side in range(2):
            copies[side][part].start()
    for copy in scalars:
        copy.start()
    lane = lax.broadcasted_iota(jnp.int32, (8, 128), 1)
    lus, rhss, u0s = [], [], []
    for side in range(2):
        copies[side][0].wait()
        copies[side][1].wait()
        e = lu([[diag_edge[side, a, b] for b in range(5)] for a in range(5)])
        rhs = [rhs_edge[side, a] for a in range(5)]
        u0 = solve(lambda a, b: e[a][b], rhs)
        lus.append(e)
        rhss.append(rhs)
        u0s.append(u0)
        edge_row = 0 if side == 0 else 7
        for a in range(5):
            token[pl.ds(TOKEN * side + a, 1)] = u0[a][edge_row : edge_row + 1]
            for b in range(5):
                factors[side, 5 * a + b] = e[a][b]
    for copy in scalars:
        copy.wait()
    count = blocks.shape[0]
    me = lax.axis_index("blk")
    before = lax.rem(me + count - 1, count)
    after = lax.rem(me + 1, count)
    first_end = blocks[before] != blocks[me]
    last_end = blocks[after] != blocks[me]
    codes = (
        jnp.where(first_end, jnp.maximum(pairs[0, 0], 0), 2 * before + 1),
        jnp.where(last_end, jnp.maximum(pairs[0, 1], 0), 2 * after),
    )
    for side in range(2):
        token[pl.ds(TOKEN * side + CODE_AT, 1)] = jnp.full(
            (1, 128), codes[side], jnp.int32
        ).astype(F32)
    for side in range(2):
        copies[side][2].wait()
        edge_row = 0 if side == 0 else 7
        half = slice(0, 8) if side == 0 else slice(8, 16)
        outer, inner = (0, 1) if side == 0 else (1, 0)

        def off(face, a, b):
            return off_edge[side, face, a, b].astype(F32)[half]

        e, u0 = lus[side], u0s[side]
        factor_at = lambda a, b: e[a][b]
        acc = list(rhss[side])
        for b in range(5):
            around = (
                (inner, pltpu.roll(u0[b], 7 if side == 0 else 1, 0)),
                (2, south(u0[b], lane)),
                (3, north(u0[b], lane)),
            )
            for face, value in around:
                for a in range(5):
                    acc[a] = acc[a] - off(face, a, b) * value
        base = solve(factor_at, acc)
        at = TOKEN * side
        for a in range(5):
            token[pl.ds(at + A_AT + a, 1)] = base[a][edge_row : edge_row + 1]
        for b in range(5):
            column = solve(factor_at, [off(outer, a, b) for a in range(5)])
            for a in range(5):
                token[pl.ds(at + M_AT + 5 * a + b, 1)] = column[a][edge_row : edge_row + 1]


def sweep_rows(source, rhs, off, factors, at, tile):
    lane = lax.broadcasted_iota(jnp.int32, (tile, 128), 1)
    here = pl.ds(at, tile)
    acc = [rhs[a, here] for a in range(5)]
    for b in range(5):
        middle = source[b, pl.ds(at + 8, tile)]
        around = (
            source[b, pl.ds(at + 7, tile)],
            source[b, pl.ds(at + 9, tile)],
            south(middle, lane),
            north(middle, lane),
        )
        for face in range(4):
            for a in range(5):
                acc[a] = acc[a] - off[face, a, b, here].astype(F32) * around[face]
    return solve(lambda a, b: factors[a, b, here], acc)


def early_kernel(token, rhs, off, diag, factors, first_sweep, upper, start):
    del token
    rows = rhs.shape[1]
    for b in range(5):
        for field in (start, first_sweep):
            field[b, 0:8] = jnp.zeros((8, 128), F32)
            field[b, 8 + rows : 16 + rows] = jnp.zeros((8, 128), F32)

    def factor_step(step, _):
        at = pl.multiple_of(step * FACTOR_TILE, FACTOR_TILE)
        here = pl.ds(at, FACTOR_TILE)
        e = lu([[diag[a, b, here] for b in range(5)] for a in range(5)])
        for a in range(5):
            for b in range(5):
                factors[a, b, here] = e[a][b]
        u0 = solve(lambda a, b: e[a][b], [rhs[a, here] for a in range(5)])
        for a in range(5):
            start[a, pl.ds(at + 8, FACTOR_TILE)] = u0[a]
        return 0

    def first_step(step, _):
        at = pl.multiple_of(step * TILE, TILE)
        fresh = sweep_rows(start, rhs, off, factors, at, TILE)
        for a in range(5):
            first_sweep[a, pl.ds(at + 8, TILE)] = fresh[a]
        return 0

    def second_step(step, _):
        at = pl.multiple_of(step * TILE, TILE)
        fresh = sweep_rows(first_sweep, rhs, off, factors, at, TILE)
        for a in range(5):
            upper[a, pl.ds(at, TILE)] = fresh[a]
        return 0

    lax.fori_loop(0, rows // FACTOR_TILE, factor_step, 0)
    lax.fori_loop(0, rows // TILE, first_step, 0)
    lax.fori_loop(0, upper.shape[1] // TILE, second_step, 0)


def late_kernel(rhs, off, factors, first_sweep, upper, out_h, lower, sems):
    done, left = upper.shape[1], lower.shape[1]
    copies = (
        pltpu.make_async_copy(upper, out_h.at[:, pl.ds(0, done)], sems.at[0]),
        pltpu.make_async_copy(lower, out_h.at[:, pl.ds(done, left)], sems.at[1]),
    )
    copies[0].start()

    def second_step(step, _):
        at = pl.multiple_of(step * TILE, TILE)
        fresh = sweep_rows(first_sweep, rhs, off, factors, done + at, TILE)
        for a in range(5):
            lower[a, pl.ds(at, TILE)] = fresh[a]
        return 0

    lax.fori_loop(0, left // TILE, second_step, 0)
    copies[1].start()
    for copy in copies:
        copy.wait()


def table(values, at):
    result = values[0]
    for k in range(1, len(values)):
        result = jnp.where(at == k, values[k], result)
    return result


def select_kernel(*refs):
    lines = len(refs) - PLANE - 1
    tokens, outs = refs[:lines], refs[lines + 1 :]
    me = lax.axis_index("blk")
    place = me % PLANE
    for out, step in zip(outs, (tuple(range(PLANE)),) + PLANE_STEPS):
        target = me - place + table(step, place)
        for slot in range(2):
            wanted = (2 * target + slot).astype(F32)
            found = jnp.zeros((TOKEN, 128), F32)
            for token in tokens:
                for side in range(2):
                    code = token[pl.ds(TOKEN * side + CODE_AT, 1)]
                    value = token[pl.ds(TOKEN * side, TOKEN)]
                    found = jnp.where(code == wanted, value, found)
            out[pl.ds(TOKEN * slot, TOKEN)] = found


def finish_kernel(*refs):
    out_in, own, *arrived = refs[: 2 + PLANE]
    order, off_edge, factors, upper, lower, out_h, beyond, result, sems = refs[2 + PLANE :]
    rows = out_h.shape[1]
    me = lax.axis_index("blk")
    lane = lax.broadcasted_iota(jnp.int32, (8, 128), 1)
    row = lax.broadcasted_iota(jnp.int32, (8, 128), 0)
    copies = []
    for side in range(2):
        at = TOKEN * side
        half = slice(0, 8) if side == 0 else slice(8, 16)
        edge_row, next_row = (0, 1) if side == 0 else (7, 6)
        outer = outer_face(side)
        source = own[pl.ds(at + CODE_AT, 1)].astype(jnp.int32) // 2
        found = arrived[0][pl.ds(at, TOKEN)]
        for value, step in zip(arrived[1:], PLANE_STEPS):
            sender = table([step.index(k) for k in range(PLANE)], me % PLANE)
            here = lax.rem(source, PLANE) == sender
            found = jnp.where(here, value[pl.ds(at, TOKEN)], found)
        columns = jnp.broadcast_to(order[0, side : side + 1], (8, 128))
        for first in (0, 8, 16, 24, TOKEN - 8):
            rows8 = found[first : first + 8]
            beyond[side, pl.ds(first, 8)] = jnp.take_along_axis(rows8, columns, axis=1)

        def mine(k):
            return own[pl.ds(at + k, 1)]

        def theirs(k):
            return beyond[side, pl.ds(k, 1)]

        def off(face, a, b):
            return off_edge[side, face, a, b].astype(F32)[half]

        acc = [jnp.zeros((8, 128), F32) for _ in range(5)]
        ahead, change = [], []
        for a in range(5):
            u1, delta = theirs(A_AT + a), jnp.zeros((1, 128), F32)
            for b in range(5):
                u1 = u1 - theirs(M_AT + 5 * a + b) * mine(b)
                delta = delta - mine(M_AT + 5 * a + b) * theirs(b)
            ahead.append(jnp.broadcast_to(u1, (8, 128)))
            change.append(jnp.broadcast_to(delta, (8, 128)))
        for b in range(5):
            at_edge = row == edge_row
            around = (
                (outer, jnp.where(at_edge, ahead[b], jnp.where(row == next_row, change[b], 0.0))),
                (2, jnp.where(at_edge, south(change[b], lane), 0.0)),
                (3, jnp.where(at_edge, north(change[b], lane), 0.0)),
            )
            for face, value in around:
                for a in range(5):
                    acc[a] = acc[a] + off(face, a, b) * value
        less = solve(lambda a, b: factors[side, 5 * a + b], acc)
        for a in range(5):
            near = upper[a, 0:8] if side == 0 else lower[a, pl.ds(lower.shape[1] - 8, 8)]
            result[side, a] = near - less[a]
        copies.append(
            pltpu.make_async_copy(
                result.at[side],
                out_h.at[:, pl.ds(0 if side == 0 else rows - 8, 8)],
                sems.at[side],
            )
        )
        copies[-1].start()
    for copy in copies:
        copy.wait()


def in_vmem(value):
    return pltpu.with_memory_space_constraint(value, VMEM)


def in_hbm(value):
    return pltpu.with_memory_space_constraint(value, pltpu.HBM)


def along_line(value, step):
    pairs = [(PLANE * k + j, PLANE * to + j) for k, to in enumerate(step) for j in range(PLANE)]
    return lax.ppermute(value, "blk", pairs)


def within_plane(value, step):
    lines = lax.axis_size("blk") // PLANE
    pairs = [(PLANE * k + j, PLANE * k + to) for k in range(lines) for j, to in enumerate(step)]
    return lax.ppermute(value, "blk", pairs)


def on_device(right_side, off_diag, diag_block, block_of_device, interface_pairs, strip_order):
    count = lax.axis_size("blk")
    rows = right_side.shape[1]
    any_space = pl.BlockSpec(memory_space=pl.ANY)
    whole = pl.BlockSpec(memory_space=VMEM)
    token, factors_edge, off_edge = pl.pallas_call(
        edge_kernel,
        out_shape=(
            VMEM((2 * TOKEN, 128), F32),
            VMEM((2, 25, 8, 128), F32),
            VMEM((2, 4, 5, 5, 16, 128), off_diag.dtype),
        ),
        in_specs=[any_space] * 5,
        out_specs=(whole, whole, whole),
        scratch_shapes=[
            pltpu.SMEM(block_of_device.shape, jnp.int32),
            pltpu.SMEM(interface_pairs.shape, jnp.int32),
            VMEM((2, 5, 8, 128), F32),
            VMEM((2, 5, 5, 8, 128), F32),
            pltpu.SemaphoreType.DMA((2, 3)),
            pltpu.SemaphoreType.DMA((2,)),
        ],
        compiler_params=pltpu.CompilerParams(vmem_limit_bytes=8 * MIB),
        name="edges",
    )(
        in_hbm(block_of_device),
        in_hbm(interface_pairs),
        in_hbm(right_side),
        in_hbm(off_diag),
        in_hbm(diag_block),
    )

    lines = count // PLANE
    if lines <= 8:
        steps = [[k ^ by for k in range(lines)] for by in range(1, lines)]
        if lines == len(LINE_STEPS[0]):
            steps = LINE_STEPS
        tokens = [token] + [along_line(token, step) for step in steps]
    else:
        groups = [[PLANE * k + j for k in range(lines)] for j in range(PLANE)]
        gathered = lax.all_gather(token, "blk", axis_index_groups=groups)
        tokens = [gathered[k] for k in range(lines)]

    rows_early = rows // 4 // TILE * TILE
    factors, first_sweep, upper = pl.pallas_call(
        early_kernel,
        out_shape=(
            VMEM((5, 5, rows, 128), F32),
            VMEM((5, rows + 16, 128), F32),
            VMEM((5, rows_early, 128), F32),
        ),
        in_specs=[any_space, whole, whole, whole],
        out_specs=(whole, whole, whole),
        scratch_shapes=[VMEM((5, rows + 16, 128), F32)],
        compiler_params=pltpu.CompilerParams(vmem_limit_bytes=12 * MIB),
        cost_estimate=pl.CostEstimate(
            flops=20000000, bytes_accessed=12 * MIB, transcendentals=0
        ),
        name="early",
    )(token, in_vmem(right_side), in_vmem(off_diag), in_vmem(diag_block))

    chosen = pl.pallas_call(
        select_kernel,
        out_shape=[VMEM((2 * TOKEN, 128), F32)] * PLANE,
        in_specs=[whole] * len(tokens) + [any_space],
        out_specs=[whole] * PLANE,
        compiler_params=pltpu.CompilerParams(vmem_limit_bytes=8 * MIB),
        name="choose",
    )(*[in_vmem(value) for value in tokens], upper)

    inside, lower = pl.pallas_call(
        late_kernel,
        out_shape=(
            pltpu.HBM(right_side.shape, F32),
            VMEM((5, rows - rows_early, 128), F32),
        ),
        in_specs=[whole] * 5,
        out_specs=(any_space, whole),
        scratch_shapes=[pltpu.SemaphoreType.DMA((2,))],
        compiler_params=pltpu.CompilerParams(vmem_limit_bytes=8 * MIB),
        cost_estimate=pl.CostEstimate(
            flops=8000000, bytes_accessed=6 * MIB, transcendentals=0
        ),
        name="late",
    )(*[in_vmem(value) for value in (right_side, off_diag, factors, first_sweep, upper)])
    arrived = [chosen[0]]
    for value, step in zip(chosen[1:], PLANE_STEPS):
        arrived.append(within_plane(value, step))

    return pl.pallas_call(
        finish_kernel,
        out_shape=pltpu.HBM(right_side.shape, F32),
        in_specs=[any_space] + [whole] * (1 + PLANE + 5),
        out_specs=any_space,
        scratch_shapes=[
            VMEM((2, TOKEN + 4, 128), F32),
            VMEM((2, 5, 8, 128), F32),
            pltpu.SemaphoreType.DMA((2,)),
        ],
        input_output_aliases={0: 0},
        compiler_params=pltpu.CompilerParams(vmem_limit_bytes=8 * MIB),
        name="finish",
    )(
        in_hbm(inside),
        in_vmem(token),
        *[in_vmem(value) for value in arrived],
        strip_order,
        in_vmem(off_edge),
        in_vmem(factors_edge),
        in_vmem(upper),
        in_vmem(lower),
    )


def solution(mesh):
    return jax.shard_map(
        on_device,
        mesh=mesh,
        in_specs=(
            P(None, ("parts", "blk"), None),
            P(None, None, None, ("parts", "blk"), None),
            P(None, None, ("parts", "blk"), None),
            P(),
            P("blk", None),
            P("blk", None, None),
        ),
        out_specs=P(None, ("parts", "blk"), None),
        check_vma=False,
    )
```

```python
import functools

import jax
import jax.numpy as jnp
from jax import lax
from jax.experimental import pallas as pl
from jax.experimental.pallas import tpu as pltpu
from jax.sharding import PartitionSpec as P

F32 = jnp.float32
VMEM = pltpu.VMEM
TOKEN = 40
A_AT, M_AT, CODE_AT = 5, 10, 35
PLANE = 4
MIB = 2**20
FACTOR_TILE, TILE = 32, 64
LINE_STEPS = ((2, 3, 1, 0), (3, 2, 0, 1), (1, 0, 3, 2))
PLANE_STEPS = ((3, 2, 1, 0), (2, 3, 0, 1), (1, 0, 3, 2))


def lu(entries):
    entries = [list(row) for row in entries]
    for pivot_at in range(5):
        inverse = 1.0 / entries[pivot_at][pivot_at]
        for row_at in range(pivot_at + 1, 5):
            scale_now = entries[row_at][pivot_at] * inverse
            entries[row_at][pivot_at] = scale_now
            for col_at in range(pivot_at + 1, 5):
                entries[row_at][col_at] = (
                    entries[row_at][col_at] - scale_now * entries[pivot_at][col_at]
                )
        entries[pivot_at][pivot_at] = inverse
    return entries


def solve(factor_at, vector):
    forward = []
    for row_at in range(5):
        running = vector[row_at]
        for col_at in range(row_at):
            running = running - factor_at(row_at, col_at) * forward[col_at]
        forward.append(running)
    result = [None] * 5
    for row_at in reversed(range(5)):
        running = forward[row_at]
        for col_at in range(row_at + 1, 5):
            running = running - factor_at(row_at, col_at) * result[col_at]
        result[row_at] = running * factor_at(row_at, row_at)
    return result


def south(value, lane):
    return jnp.where(lane == 0, 0.0, pltpu.roll(value, 1, 1))


def north(value, lane):
    return jnp.where(lane == 127, 0.0, pltpu.roll(value, 127, 1))


def outer_face(side):
    return side


def edge_kernel(
    blocks_h,
    pairs_h,
    rhs_h,
    off_h,
    diag_h,
    token,
    factors,
    off_edge,
    blocks,
    pairs,
    rhs_edge,
    diag_edge,
    sems,
    scalar_sems,
):
    rows = rhs_h.shape[1]
    scalars = (
        pltpu.make_async_copy(blocks_h, blocks, scalar_sems.at[0]),
        pltpu.make_async_copy(pairs_h, pairs, scalar_sems.at[1]),
    )
    copies = []
    for side in range(2):
        at8, at16 = (0, 0) if side == 0 else (rows - 8, rows - 16)
        copies.append(
            (
                pltpu.make_async_copy(
                    diag_h.at[:, :, pl.ds(at8, 8)], diag_edge.at[side], sems.at[side, 0]
                ),
                pltpu.make_async_copy(
                    rhs_h.at[:, pl.ds(at8, 8)], rhs_edge.at[side], sems.at[side, 1]
                ),
                pltpu.make_async_copy(
                    off_h.at[:, :, :, pl.ds(at16, 16)], off_edge.at[side], sems.at[side, 2]
                ),
            )
        )
    for part in range(3):
        for side in range(2):
            copies[side][part].start()
    for copy in scalars:
        copy.start()
    lane = lax.broadcasted_iota(jnp.int32, (8, 128), 1)
    lus, rhss, u0s = [], [], []
    for side in range(2):
        copies[side][0].wait()
        copies[side][1].wait()
        e = lu([[diag_edge[side, a, b] for b in range(5)] for a in range(5)])
        rhs = [rhs_edge[side, a] for a in range(5)]
        u0 = solve(lambda a, b: e[a][b], rhs)
        lus.append(e)
        rhss.append(rhs)
        u0s.append(u0)
        edge_row = 0 if side == 0 else 7
        for a in range(5):
            token[pl.ds(TOKEN * side + a, 1)] = u0[a][edge_row : edge_row + 1]
            for b in range(5):
                factors[side, 5 * a + b] = e[a][b]
        token[pl.ds(TOKEN * side + CODE_AT + 1, TOKEN - CODE_AT - 1)] = jnp.zeros(
            (TOKEN - CODE_AT - 1, 128), F32
        )
    for copy in scalars:
        copy.wait()
    count = blocks.shape[0]
    me = lax.axis_index("blk")
    before = lax.rem(me + count - 1, count)
    after = lax.rem(me + 1, count)
    first_end = blocks[before] != blocks[me]
    last_end = blocks[after] != blocks[me]
    codes = (
        jnp.where(first_end, jnp.maximum(pairs[0, 0], 0), 2 * before + 1),
        jnp.where(last_end, jnp.maximum(pairs[0, 1], 0), 2 * after),
    )
    for side in range(2):
        token[pl.ds(TOKEN * side + CODE_AT, 1)] = jnp.full(
            (1, 128), codes[side], jnp.int32
        ).astype(F32)
    for side in range(2):
        copies[side][2].wait()
        edge_row = 0 if side == 0 else 7
        half = slice(0, 8) if side == 0 else slice(8, 16)
        outer, inner = (0, 1) if side == 0 else (1, 0)

        def off(face, a, b):
            return off_edge[side, face, a, b].astype(F32)[half]

        e, u0 = lus[side], u0s[side]
        factor_at = lambda a, b: e[a][b]
        acc = list(rhss[side])
        for b in range(5):
            around = (
                (inner, pltpu.roll(u0[b], 7 if side == 0 else 1, 0)),
                (2, south(u0[b], lane)),
                (3, north(u0[b], lane)),
            )
            for face, value in around:
                for a in range(5):
                    acc[a] = acc[a] - off(face, a, b) * value
        base = solve(factor_at, acc)
        at = TOKEN * side
        for a in range(5):
            token[pl.ds(at + A_AT + a, 1)] = base[a][edge_row : edge_row + 1]
        for b in range(5):
            column = solve(factor_at, [off(outer, a, b) for a in range(5)])
            for a in range(5):
                token[pl.ds(at + M_AT + 5 * a + b, 1)] = column[a][edge_row : edge_row + 1]


def sweep_rows(source, rhs, off, factors, at, tile):
    lane = lax.broadcasted_iota(jnp.int32, (tile, 128), 1)
    here = pl.ds(at, tile)
    acc = [rhs[a, here] for a in range(5)]
    for b in range(5):
        middle = source[b, pl.ds(at + 8, tile)]
        around = (
            source[b, pl.ds(at + 7, tile)],
            source[b, pl.ds(at + 9, tile)],
            south(middle, lane),
            north(middle, lane),
        )
        for face in range(4):
            for a in range(5):
                acc[a] = acc[a] - off[face, a, b, here].astype(F32) * around[face]
    return solve(lambda a, b: factors[a, b, here], acc)


def early_kernel(token, rhs, off, diag, factors, first_sweep, upper, start):
    del token
    rows = rhs.shape[1]
    for b in range(5):
        for field in (start, first_sweep):
            field[b, 0:8] = jnp.zeros((8, 128), F32)
            field[b, 8 + rows : 16 + rows] = jnp.zeros((8, 128), F32)

    def factor_step(step, _):
        at = pl.multiple_of(step * FACTOR_TILE, FACTOR_TILE)
        here = pl.ds(at, FACTOR_TILE)
        e = lu([[diag[a, b, here] for b in range(5)] for a in range(5)])
        for a in range(5):
            for b in range(5):
                factors[a, b, here] = e[a][b]
        u0 = solve(lambda a, b: e[a][b], [rhs[a, here] for a in range(5)])
        for a in range(5):
            start[a, pl.ds(at + 8, FACTOR_TILE)] = u0[a]
        return 0

    def first_step(step, _):
        at = pl.multiple_of(step * TILE, TILE)
        fresh = sweep_rows(start, rhs, off, factors, at, TILE)
        for a in range(5):
            first_sweep[a, pl.ds(at + 8, TILE)] = fresh[a]
        return 0

    def second_step(step, _):
        at = pl.multiple_of(step * TILE, TILE)
        fresh = sweep_rows(first_sweep, rhs, off, factors, at, TILE)
        for a in range(5):
            upper[a, pl.ds(at, TILE)] = fresh[a]
        return 0

    lax.fori_loop(0, rows // FACTOR_TILE, factor_step, 0)
    lax.fori_loop(0, rows // TILE, first_step, 0)
    lax.fori_loop(0, upper.shape[1] // TILE, second_step, 0)


def late_kernel(rhs, off, factors, first_sweep, upper, out_h, lower, sems):
    done, left = upper.shape[1], lower.shape[1]
    copies = (
        pltpu.make_async_copy(upper, out_h.at[:, pl.ds(0, done)], sems.at[0]),
        pltpu.make_async_copy(lower, out_h.at[:, pl.ds(done, left)], sems.at[1]),
    )
    copies[0].start()

    def second_step(step, _):
        at = pl.multiple_of(step * TILE, TILE)
        fresh = sweep_rows(first_sweep, rhs, off, factors, done + at, TILE)
        for a in range(5):
            lower[a, pl.ds(at, TILE)] = fresh[a]
        return 0

    lax.fori_loop(0, left // TILE, second_step, 0)
    copies[1].start()
    for copy in copies:
        copy.wait()


def table(values, at):
    result = values[0]
    for k in range(1, len(values)):
        result = jnp.where(at == k, values[k], result)
    return result


def select_kernel(*refs):
    lines = len(refs) - PLANE - 1
    tokens, outs = refs[:lines], refs[lines + 1 :]
    me = lax.axis_index("blk")
    place = me % PLANE
    for out, step in zip(outs, (tuple(range(PLANE)),) + PLANE_STEPS):
        target = me - place + table(step, place)
        for slot in range(2):
            wanted = (2 * target + slot).astype(F32)
            found = jnp.zeros((TOKEN, 128), F32)
            for token in tokens:
                for side in range(2):
                    code = token[pl.ds(TOKEN * side + CODE_AT, 1)]
                    value = token[pl.ds(TOKEN * side, TOKEN)]
                    found = jnp.where(code == wanted, value, found)
            out[pl.ds(TOKEN * slot, TOKEN)] = found


def finish_kernel(*refs):
    out_in, own, *arrived = refs[: 2 + PLANE]
    order, off_edge, factors, upper, lower, out_h, beyond, result, sems = refs[2 + PLANE :]
    rows = out_h.shape[1]
    me = lax.axis_index("blk")
    lane = lax.broadcasted_iota(jnp.int32, (8, 128), 1)
    row = lax.broadcasted_iota(jnp.int32, (8, 128), 0)
    copies = []
    for side in range(2):
        at = TOKEN * side
        half = slice(0, 8) if side == 0 else slice(8, 16)
        edge_row, next_row = (0, 1) if side == 0 else (7, 6)
        outer = outer_face(side)
        source = own[pl.ds(at + CODE_AT, 1)].astype(jnp.int32) // 2
        found = arrived[0][pl.ds(at, TOKEN)]
        for value, step in zip(arrived[1:], PLANE_STEPS):
            sender = table([step.index(k) for k in range(PLANE)], me % PLANE)
            here = lax.rem(source, PLANE) == sender
            found = jnp.where(here, value[pl.ds(at, TOKEN)], found)
        columns = jnp.broadcast_to(order[0, side : side + 1], (TOKEN, 128))
        beyond[side] = jnp.take_along_axis(found, columns, axis=1)

        def mine(k):
            return own[pl.ds(at + k, 1)]

        def theirs(k):
            return beyond[side, pl.ds(k, 1)]

        def off(face, a, b):
            return off_edge[side, face, a, b].astype(F32)[half]

        acc = [jnp.zeros((8, 128), F32) for _ in range(5)]
        ahead, change = [], []
        for a in range(5):
            u1, delta = theirs(A_AT + a), jnp.zeros((1, 128), F32)
            for b in range(5):
                u1 = u1 - theirs(M_AT + 5 * a + b) * mine(b)
                delta = delta - mine(M_AT + 5 * a + b) * theirs(b)
            ahead.append(jnp.broadcast_to(u1, (8, 128)))
            change.append(jnp.broadcast_to(delta, (8, 128)))
        for b in range(5):
            at_edge = row == edge_row
            around = (
                (outer, jnp.where(at_edge, ahead[b], jnp.where(row == next_row, change[b], 0.0))),
                (2, jnp.where(at_edge, south(change[b], lane), 0.0)),
                (3, jnp.where(at_edge, north(change[b], lane), 0.0)),
            )
            for face, value in around:
                for a in range(5):
                    acc[a] = acc[a] + off(face, a, b) * value
        less = solve(lambda a, b: factors[side, 5 * a + b], acc)
        for a in range(5):
            near = upper[a, 0:8] if side == 0 else lower[a, pl.ds(lower.shape[1] - 8, 8)]
            result[side, a] = near - less[a]
        copies.append(
            pltpu.make_async_copy(
                result.at[side],
                out_h.at[:, pl.ds(0 if side == 0 else rows - 8, 8)],
                sems.at[side],
            )
        )
        copies[-1].start()
    for copy in copies:
        copy.wait()


def in_vmem(value):
    return pltpu.with_memory_space_constraint(value, VMEM)


def in_hbm(value):
    return pltpu.with_memory_space_constraint(value, pltpu.HBM)


def along_line(value, step):
    pairs = [(PLANE * k + j, PLANE * to + j) for k, to in enumerate(step) for j in range(PLANE)]
    return lax.ppermute(value, "blk", pairs)


def within_plane(value, step):
    lines = lax.axis_size("blk") // PLANE
    pairs = [(PLANE * k + j, PLANE * k + to) for k in range(lines) for j, to in enumerate(step)]
    return lax.ppermute(value, "blk", pairs)


def on_device(right_side, off_diag, diag_block, block_of_device, interface_pairs, strip_order):
    count = lax.axis_size("blk")
    rows = right_side.shape[1]
    any_space = pl.BlockSpec(memory_space=pl.ANY)
    whole = pl.BlockSpec(memory_space=VMEM)
    token, factors_edge, off_edge = pl.pallas_call(
        edge_kernel,
        out_shape=(
            VMEM((2 * TOKEN, 128), F32),
            VMEM((2, 25, 8, 128), F32),
            VMEM((2, 4, 5, 5, 16, 128), off_diag.dtype),
        ),
        in_specs=[any_space] * 5,
        out_specs=(whole, whole, whole),
        scratch_shapes=[
            pltpu.SMEM(block_of_device.shape, jnp.int32),
            pltpu.SMEM(interface_pairs.shape, jnp.int32),
            VMEM((2, 5, 8, 128), F32),
            VMEM((2, 5, 5, 8, 128), F32),
            pltpu.SemaphoreType.DMA((2, 3)),
            pltpu.SemaphoreType.DMA((2,)),
        ],
        compiler_params=pltpu.CompilerParams(vmem_limit_bytes=8 * MIB),
        name="edges",
    )(
        in_hbm(block_of_device),
        in_hbm(interface_pairs),
        in_hbm(right_side),
        in_hbm(off_diag),
        in_hbm(diag_block),
    )

    lines = count // PLANE
    if lines <= 8:
        steps = [[k ^ by for k in range(lines)] for by in range(1, lines)]
        if lines == len(LINE_STEPS[0]):
            steps = LINE_STEPS
        tokens = [token] + [along_line(token, step) for step in steps]
    else:
        groups = [[PLANE * k + j for k in range(lines)] for j in range(PLANE)]
        gathered = lax.all_gather(token, "blk", axis_index_groups=groups)
        tokens = [gathered[k] for k in range(lines)]

    rows_early = rows // 4 // TILE * TILE
    factors, first_sweep, upper = pl.pallas_call(
        early_kernel,
        out_shape=(
            VMEM((5, 5, rows, 128), F32),
            VMEM((5, rows + 16, 128), F32),
            VMEM((5, rows_early, 128), F32),
        ),
        in_specs=[any_space, whole, whole, whole],
        out_specs=(whole, whole, whole),
        scratch_shapes=[VMEM((5, rows + 16, 128), F32)],
        compiler_params=pltpu.CompilerParams(vmem_limit_bytes=12 * MIB),
        cost_estimate=pl.CostEstimate(
            flops=20000000, bytes_accessed=12 * MIB, transcendentals=0
        ),
        name="early",
    )(token, in_vmem(right_side), in_vmem(off_diag), in_vmem(diag_block))

    chosen = pl.pallas_call(
        select_kernel,
        out_shape=[VMEM((2 * TOKEN, 128), F32)] * PLANE,
        in_specs=[whole] * len(tokens) + [any_space],
        out_specs=[whole] * PLANE,
        compiler_params=pltpu.CompilerParams(vmem_limit_bytes=8 * MIB),
        name="choose",
    )(*[in_vmem(value) for value in tokens], upper)

    inside, lower = pl.pallas_call(
        late_kernel,
        out_shape=(
            pltpu.HBM(right_side.shape, F32),
            VMEM((5, rows - rows_early, 128), F32),
        ),
        in_specs=[whole] * 5,
        out_specs=(any_space, whole),
        scratch_shapes=[pltpu.SemaphoreType.DMA((2,))],
        compiler_params=pltpu.CompilerParams(vmem_limit_bytes=8 * MIB),
        cost_estimate=pl.CostEstimate(
            flops=8000000, bytes_accessed=6 * MIB, transcendentals=0
        ),
        name="late",
    )(*[in_vmem(value) for value in (right_side, off_diag, factors, first_sweep, upper)])
    arrived = [chosen[0]]
    for value, step in zip(chosen[1:], PLANE_STEPS):
        arrived.append(within_plane(value, step))

    return pl.pallas_call(
        finish_kernel,
        out_shape=pltpu.HBM(right_side.shape, F32),
        in_specs=[any_space] + [whole] * (1 + PLANE + 5),
        out_specs=any_space,
        scratch_shapes=[
            VMEM((2, TOKEN, 128), F32),
            VMEM((2, 5, 8, 128), F32),
            pltpu.SemaphoreType.DMA((2,)),
        ],
        input_output_aliases={0: 0},
        compiler_params=pltpu.CompilerParams(vmem_limit_bytes=8 * MIB),
        name="finish",
    )(
        in_hbm(inside),
        in_vmem(token),
        *[in_vmem(value) for value in arrived],
        strip_order,
        in_vmem(off_edge),
        in_vmem(factors_edge),
        in_vmem(upper),
        in_vmem(lower),
    )


def solution(mesh):
    return jax.shard_map(
        on_device,
        mesh=mesh,
        in_specs=(
            P(None, ("parts", "blk"), None),
            P(None, None, None, ("parts", "blk"), None),
            P(None, None, ("parts", "blk"), None),
            P(),
            P("blk", None),
            P("blk", None, None),
        ),
        out_specs=P(None, ("parts", "blk"), None),
        check_vma=False,
    )
```

```python
import functools

import jax
import jax.numpy as jnp
from jax import lax
from jax.experimental import pallas as pl
from jax.experimental.pallas import tpu as pltpu
from jax.sharding import PartitionSpec as P

F32 = jnp.float32
VMEM = pltpu.VMEM
TOKEN = 36
A_AT, M_AT, CODE_AT = 5, 10, 35
PLANE = 4
MIB = 2**20
FACTOR_TILE, TILE = 64, 64
LINE_STEPS = ((2, 3, 1, 0), (3, 2, 0, 1), (1, 0, 3, 2))
LINE_FLIPS = (1, 1, 1)
PLANE_STEPS = ((3, 2, 0, 1), (2, 3, 1, 0), (1, 0, 3, 2))


def lu(entries):
    entries = [list(row) for row in entries]
    for pivot_at in range(5):
        inverse = 1.0 / entries[pivot_at][pivot_at]
        for row_at in range(pivot_at + 1, 5):
            scale_now = entries[row_at][pivot_at] * inverse
            entries[row_at][pivot_at] = scale_now
            for col_at in range(pivot_at + 1, 5):
                entries[row_at][col_at] = (
                    entries[row_at][col_at] - scale_now * entries[pivot_at][col_at]
                )
        entries[pivot_at][pivot_at] = inverse
    return entries


def solve(factor_at, vector):
    forward = []
    for row_at in range(5):
        running = vector[row_at]
        for col_at in range(row_at):
            running = running - factor_at(row_at, col_at) * forward[col_at]
        forward.append(running)
    result = [None] * 5
    for row_at in reversed(range(5)):
        running = forward[row_at]
        for col_at in range(row_at + 1, 5):
            running = running - factor_at(row_at, col_at) * result[col_at]
        result[row_at] = running * factor_at(row_at, row_at)
    return result


def south(value, lane):
    return jnp.where(lane == 0, 0.0, pltpu.roll(value, 1, 1))


def north(value, lane):
    return jnp.where(lane == 127, 0.0, pltpu.roll(value, 127, 1))


def outer_face(side):
    return side


def edge_kernel(
    blocks_h,
    pairs_h,
    rhs_h,
    off_h,
    diag_h,
    token,
    factors,
    off_edge,
    blocks,
    pairs,
    rhs_edge,
    diag_edge,
    sems,
    scalar_sems,
):
    rows = rhs_h.shape[1]
    scalars = (
        pltpu.make_async_copy(blocks_h, blocks, scalar_sems.at[0]),
        pltpu.make_async_copy(pairs_h, pairs, scalar_sems.at[1]),
    )
    copies = []
    for side in range(2):
        at8, at16 = (0, 0) if side == 0 else (rows - 8, rows - 16)
        copies.append(
            (
                pltpu.make_async_copy(
                    diag_h.at[:, :, pl.ds(at8, 8)], diag_edge.at[side], sems.at[side, 0]
                ),
                pltpu.make_async_copy(
                    rhs_h.at[:, pl.ds(at8, 8)], rhs_edge.at[side], sems.at[side, 1]
                ),
                pltpu.make_async_copy(
                    off_h.at[:, :, :, pl.ds(at16, 16)], off_edge.at[side], sems.at[side, 2]
                ),
            )
        )
    for part in range(3):
        for side in range(2):
            copies[side][part].start()
    for copy in scalars:
        copy.start()
    lane = lax.broadcasted_iota(jnp.int32, (8, 128), 1)
    lus, rhss, u0s = [], [], []
    for side in range(2):
        copies[side][0].wait()
        copies[side][1].wait()
        e = lu([[diag_edge[side, a, b] for b in range(5)] for a in range(5)])
        rhs = [rhs_edge[side, a] for a in range(5)]
        u0 = solve(lambda a, b: e[a][b], rhs)
        lus.append(e)
        rhss.append(rhs)
        u0s.append(u0)
        edge_row = 0 if side == 0 else 7
        for a in range(5):
            token[pl.ds(TOKEN * side + a, 1)] = u0[a][edge_row : edge_row + 1]
            for b in range(5):
                factors[side, 5 * a + b] = e[a][b]
    for copy in scalars:
        copy.wait()
    count = blocks.shape[0]
    me = lax.axis_index("blk")
    before = lax.rem(me + count - 1, count)
    after = lax.rem(me + 1, count)
    first_end = blocks[before] != blocks[me]
    last_end = blocks[after] != blocks[me]
    codes = (
        jnp.where(first_end, jnp.maximum(pairs[0, 0], 0), 2 * before + 1),
        jnp.where(last_end, jnp.maximum(pairs[0, 1], 0), 2 * after),
    )
    for side in range(2):
        token[pl.ds(TOKEN * side + CODE_AT, 1)] = jnp.full(
            (1, 128), codes[side], jnp.int32
        ).astype(F32)
    for side in range(2):
        copies[side][2].wait()
        edge_row = 0 if side == 0 else 7
        half = slice(0, 8) if side == 0 else slice(8, 16)
        outer, inner = (0, 1) if side == 0 else (1, 0)

        def off(face, a, b):
            return off_edge[side, face, a, b].astype(F32)[half]

        e, u0 = lus[side], u0s[side]
        factor_at = lambda a, b: e[a][b]
        acc = list(rhss[side])
        for b in range(5):
            around = (
                (inner, pltpu.roll(u0[b], 7 if side == 0 else 1, 0)),
                (2, south(u0[b], lane)),
                (3, north(u0[b], lane)),
            )
            for face, value in around:
                for a in range(5):
                    acc[a] = acc[a] - off(face, a, b) * value
        base = solve(factor_at, acc)
        at = TOKEN * side
        for a in range(5):
            token[pl.ds(at + A_AT + a, 1)] = base[a][edge_row : edge_row + 1]
        for b in range(5):
            column = solve(factor_at, [off(outer, a, b) for a in range(5)])
            for a in range(5):
                token[pl.ds(at + M_AT + 5 * a + b, 1)] = column[a][edge_row : edge_row + 1]


def sweep_rows(source, rhs, off, factors, at, tile):
    lane = lax.broadcasted_iota(jnp.int32, (tile, 128), 1)
    here = pl.ds(at, tile)
    acc = [rhs[a, here] for a in range(5)]
    for b in range(5):
        middle = source[b, pl.ds(at + 8, tile)]
        around = (
            source[b, pl.ds(at + 7, tile)],
            source[b, pl.ds(at + 9, tile)],
            south(middle, lane),
            north(middle, lane),
        )
        for face in range(4):
            for a in range(5):
                acc[a] = acc[a] - off[face, a, b, here].astype(F32) * around[face]
    return solve(lambda a, b: factors[a, b, here], acc)


def early_kernel(token, rhs, off, diag, factors, first_sweep, upper, start):
    del token
    rows = rhs.shape[1]
    for b in range(5):
        for field in (start, first_sweep):
            field[b, 0:8] = jnp.zeros((8, 128), F32)
            field[b, 8 + rows : 16 + rows] = jnp.zeros((8, 128), F32)

    def factor_step(step, _):
        at = pl.multiple_of(step * FACTOR_TILE, FACTOR_TILE)
        here = pl.ds(at, FACTOR_TILE)
        e = lu([[diag[a, b, here] for b in range(5)] for a in range(5)])
        for a in range(5):
            for b in range(5):
                factors[a, b, here] = e[a][b]
        u0 = solve(lambda a, b: e[a][b], [rhs[a, here] for a in range(5)])
        for a in range(5):
            start[a, pl.ds(at + 8, FACTOR_TILE)] = u0[a]
        return 0

    def first_step(step, _):
        at = pl.multiple_of(step * TILE, TILE)
        fresh = sweep_rows(start, rhs, off, factors, at, TILE)
        for a in range(5):
            first_sweep[a, pl.ds(at + 8, TILE)] = fresh[a]
        return 0

    def second_step(step, _):
        at = pl.multiple_of(step * TILE, TILE)
        fresh = sweep_rows(first_sweep, rhs, off, factors, at, TILE)
        for a in range(5):
            upper[a, pl.ds(at, TILE)] = fresh[a]
        return 0

    lax.fori_loop(0, rows // FACTOR_TILE, factor_step, 0)
    lax.fori_loop(0, rows // TILE, first_step, 0)
    lax.fori_loop(0, upper.shape[1] // TILE, second_step, 0)


def late_kernel(rhs, off, factors, first_sweep, upper, out_h, lower, sems):
    done, left = upper.shape[1], lower.shape[1]
    copies = (
        pltpu.make_async_copy(upper, out_h.at[:, pl.ds(0, done)], sems.at[0]),
        pltpu.make_async_copy(lower, out_h.at[:, pl.ds(done, left)], sems.at[1]),
    )
    copies[0].start()

    def second_step(step, _):
        at = pl.multiple_of(step * TILE, TILE)
        fresh = sweep_rows(first_sweep, rhs, off, factors, done + at, TILE)
        for a in range(5):
            lower[a, pl.ds(at, TILE)] = fresh[a]
        return 0

    lax.fori_loop(0, left // TILE, second_step, 0)
    copies[1].start()
    for copy in copies:
        copy.wait()


def table(values, at):
    result = values[0]
    for k in range(1, len(values)):
        result = jnp.where(at == k, values[k], result)
    return result


def select_kernel(*refs):
    lines = len(refs) - PLANE - 1
    tokens, outs = refs[:lines], refs[lines + 1 :]
    me = lax.axis_index("blk")
    place = me % PLANE
    for out, step in zip(outs, (tuple(range(PLANE)),) + PLANE_STEPS):
        target = me - place + table(step, place)
        for slot in range(2):
            wanted = (2 * target + slot).astype(F32)
            found = jnp.full((TOKEN, 128), -1.0, F32)
            for token in tokens:
                for side in range(2):
                    code = token[pl.ds(TOKEN * side + CODE_AT, 1)]
                    value = token[pl.ds(TOKEN * side, TOKEN)]
                    found = jnp.where(code == wanted, value, found)
            out[pl.ds(TOKEN * slot, TOKEN)] = found


def finish_kernel(*refs):
    out_in, own, *arrived = refs[: 2 + PLANE]
    order, off_edge, factors, upper, lower, out_h, beyond, result, sems = refs[2 + PLANE :]
    rows = out_h.shape[1]
    me = lax.axis_index("blk")
    lane = lax.broadcasted_iota(jnp.int32, (8, 128), 1)
    row = lax.broadcasted_iota(jnp.int32, (8, 128), 0)
    copies = []
    for side in range(2):
        at = TOKEN * side
        half = slice(0, 8) if side == 0 else slice(8, 16)
        edge_row, next_row = (0, 1) if side == 0 else (7, 6)
        outer = outer_face(side)
        found = arrived[0][pl.ds(at, TOKEN)]
        for value in arrived[1:]:
            here = value[pl.ds(at + CODE_AT, 1)] == (2 * me + side).astype(F32)
            found = jnp.where(here, value[pl.ds(at, TOKEN)], found)
        columns = jnp.broadcast_to(order[0, side : side + 1], (8, 128))
        for first in (0, 8, 16, 24, TOKEN - 8):
            rows8 = found[first : first + 8]
            beyond[side, pl.ds(first, 8)] = jnp.take_along_axis(rows8, columns, axis=1)

        def mine(k):
            return own[pl.ds(at + k, 1)]

        def theirs(k):
            return beyond[side, pl.ds(k, 1)]

        def off(face, a, b):
            return off_edge[side, face, a, b].astype(F32)[half]

        acc = [jnp.zeros((8, 128), F32) for _ in range(5)]
        ahead, change = [], []
        for a in range(5):
            u1, delta = theirs(A_AT + a), jnp.zeros((1, 128), F32)
            for b in range(5):
                u1 = u1 - theirs(M_AT + 5 * a + b) * mine(b)
                delta = delta - mine(M_AT + 5 * a + b) * theirs(b)
            ahead.append(jnp.broadcast_to(u1, (8, 128)))
            change.append(jnp.broadcast_to(delta, (8, 128)))
        for b in range(5):
            at_edge = row == edge_row
            around = (
                (outer, jnp.where(at_edge, ahead[b], jnp.where(row == next_row, change[b], 0.0))),
                (2, jnp.where(at_edge, south(change[b], lane), 0.0)),
                (3, jnp.where(at_edge, north(change[b], lane), 0.0)),
            )
            for face, value in around:
                for a in range(5):
                    acc[a] = acc[a] + off(face, a, b) * value
        less = solve(lambda a, b: factors[side, 5 * a + b], acc)
        for a in range(5):
            near = upper[a, 0:8] if side == 0 else lower[a, pl.ds(lower.shape[1] - 8, 8)]
            result[side, a] = near - less[a]
        copies.append(
            pltpu.make_async_copy(
                result.at[side],
                out_h.at[:, pl.ds(0 if side == 0 else rows - 8, 8)],
                sems.at[side],
            )
        )
        copies[-1].start()
    for copy in copies:
        copy.wait()


def in_vmem(value):
    return pltpu.with_memory_space_constraint(value, VMEM)


def in_hbm(value):
    return pltpu.with_memory_space_constraint(value, pltpu.HBM)


def along_line(value, step, flip):
    pairs = []
    for k, to in enumerate(step):
        pairs += [(PLANE * k + j, PLANE * to + (j ^ flip)) for j in range(PLANE)]
    return lax.ppermute(value, "blk", pairs)


def within_plane(value, step):
    lines = lax.axis_size("blk") // PLANE
    pairs = [(PLANE * k + j, PLANE * k + to) for k in range(lines) for j, to in enumerate(step)]
    return lax.ppermute(value, "blk", pairs)


def on_device(right_side, off_diag, diag_block, block_of_device, interface_pairs, strip_order):
    count = lax.axis_size("blk")
    rows = right_side.shape[1]
    any_space = pl.BlockSpec(memory_space=pl.ANY)
    whole = pl.BlockSpec(memory_space=VMEM)
    token, factors_edge, off_edge = pl.pallas_call(
        edge_kernel,
        out_shape=(
            VMEM((2 * TOKEN, 128), F32),
            VMEM((2, 25, 8, 128), F32),
            VMEM((2, 4, 5, 5, 16, 128), off_diag.dtype),
        ),
        in_specs=[any_space] * 5,
        out_specs=(whole, whole, whole),
        scratch_shapes=[
            pltpu.SMEM(block_of_device.shape, jnp.int32),
            pltpu.SMEM(interface_pairs.shape, jnp.int32),
            VMEM((2, 5, 8, 128), F32),
            VMEM((2, 5, 5, 8, 128), F32),
            pltpu.SemaphoreType.DMA((2, 3)),
            pltpu.SemaphoreType.DMA((2,)),
        ],
        compiler_params=pltpu.CompilerParams(vmem_limit_bytes=8 * MIB),
        name="edges",
    )(
        in_hbm(block_of_device),
        in_hbm(interface_pairs),
        in_hbm(right_side),
        in_hbm(off_diag),
        in_hbm(diag_block),
    )

    lines = count // PLANE
    if lines <= 8:
        steps = [([k ^ by for k in range(lines)], 0) for by in range(1, lines)]
        if lines == len(LINE_STEPS[0]):
            steps = zip(LINE_STEPS, LINE_FLIPS)
        tokens = [token] + [along_line(token, step, flip) for step, flip in steps]
    else:
        groups = [[PLANE * k + j for k in range(lines)] for j in range(PLANE)]
        gathered = lax.all_gather(token, "blk", axis_index_groups=groups)
        tokens = [gathered[k] for k in range(lines)]

    rows_early = rows // 4 // TILE * TILE
    factors, first_sweep, upper = pl.pallas_call(
        early_kernel,
        out_shape=(
            VMEM((5, 5, rows, 128), F32),
            VMEM((5, rows + 16, 128), F32),
            VMEM((5, rows_early, 128), F32),
        ),
        in_specs=[any_space, whole, whole, whole],
        out_specs=(whole, whole, whole),
        scratch_shapes=[VMEM((5, rows + 16, 128), F32)],
        compiler_params=pltpu.CompilerParams(vmem_limit_bytes=12 * MIB),
        cost_estimate=pl.CostEstimate(
            flops=20000000, bytes_accessed=12 * MIB, transcendentals=0
        ),
        name="early",
    )(token, in_vmem(right_side), in_vmem(off_diag), in_vmem(diag_block))

    chosen = pl.pallas_call(
        select_kernel,
        out_shape=[VMEM((2 * TOKEN, 128), F32)] * PLANE,
        in_specs=[whole] * len(tokens) + [any_space],
        out_specs=[whole] * PLANE,
        compiler_params=pltpu.CompilerParams(vmem_limit_bytes=8 * MIB),
        name="choose",
    )(*[in_vmem(value) for value in tokens], upper)

    inside, lower = pl.pallas_call(
        late_kernel,
        out_shape=(
            pltpu.HBM(right_side.shape, F32),
            VMEM((5, rows - rows_early, 128), F32),
        ),
        in_specs=[whole] * 5,
        out_specs=(any_space, whole),
        scratch_shapes=[pltpu.SemaphoreType.DMA((2,))],
        compiler_params=pltpu.CompilerParams(vmem_limit_bytes=8 * MIB),
        cost_estimate=pl.CostEstimate(
            flops=8000000, bytes_accessed=6 * MIB, transcendentals=0
        ),
        name="late",
    )(*[in_vmem(value) for value in (right_side, off_diag, factors, first_sweep, upper)])
    arrived = [chosen[0]]
    for value, step in zip(chosen[1:], PLANE_STEPS):
        arrived.append(within_plane(value, step))

    return pl.pallas_call(
        finish_kernel,
        out_shape=pltpu.HBM(right_side.shape, F32),
        in_specs=[any_space] + [whole] * (1 + PLANE + 5),
        out_specs=any_space,
        scratch_shapes=[
            VMEM((2, TOKEN + 4, 128), F32),
            VMEM((2, 5, 8, 128), F32),
            pltpu.SemaphoreType.DMA((2,)),
        ],
        input_output_aliases={0: 0},
        compiler_params=pltpu.CompilerParams(vmem_limit_bytes=8 * MIB),
        name="finish",
    )(
        in_hbm(inside),
        in_vmem(token),
        *[in_vmem(value) for value in arrived],
        strip_order,
        in_vmem(off_edge),
        in_vmem(factors_edge),
        in_vmem(upper),
        in_vmem(lower),
    )


def solution(mesh):
    return jax.shard_map(
        on_device,
        mesh=mesh,
        in_specs=(
            P(None, ("parts", "blk"), None),
            P(None, None, None, ("parts", "blk"), None),
            P(None, None, ("parts", "blk"), None),
            P(),
            P("blk", None),
            P("blk", None, None),
        ),
        out_specs=P(None, ("parts", "blk"), None),
        check_vma=False,
    )
```

```python
import functools

import jax
import jax.numpy as jnp
from jax import lax
from jax.experimental import pallas as pl
from jax.experimental.pallas import tpu as pltpu
from jax.sharding import PartitionSpec as P

F32 = jnp.float32
VMEM = pltpu.VMEM
TOKEN = 36
A_AT, M_AT, CODE_AT = 5, 10, 35
PLANE = 4
MIB = 2**20
FACTOR_TILE, TILE = 128, 64
LINE_STEPS = ((2, 3, 1, 0), (3, 2, 0, 1), (1, 0, 3, 2))
LINE_FLIPS = (1, 1, 1)
PLANE_STEPS = ((3, 2, 0, 1), (2, 3, 1, 0), (1, 0, 3, 2))


def lu(entries):
    entries = [list(row) for row in entries]
    for pivot_at in range(5):
        inverse = 1.0 / entries[pivot_at][pivot_at]
        for row_at in range(pivot_at + 1, 5):
            scale_now = entries[row_at][pivot_at] * inverse
            entries[row_at][pivot_at] = scale_now
            for col_at in range(pivot_at + 1, 5):
                entries[row_at][col_at] = (
                    entries[row_at][col_at] - scale_now * entries[pivot_at][col_at]
                )
        entries[pivot_at][pivot_at] = inverse
    return entries


def solve(factor_at, vector):
    forward = []
    for row_at in range(5):
        running = vector[row_at]
        for col_at in range(row_at):
            running = running - factor_at(row_at, col_at) * forward[col_at]
        forward.append(running)
    result = [None] * 5
    for row_at in reversed(range(5)):
        running = forward[row_at]
        for col_at in range(row_at + 1, 5):
            running = running - factor_at(row_at, col_at) * result[col_at]
        result[row_at] = running * factor_at(row_at, row_at)
    return result


def south(value, lane):
    return jnp.where(lane == 0, 0.0, pltpu.roll(value, 1, 1))


def north(value, lane):
    return jnp.where(lane == 127, 0.0, pltpu.roll(value, 127, 1))


def outer_face(side):
    return side


def edge_kernel(
    blocks_h,
    pairs_h,
    rhs_h,
    off_h,
    diag_h,
    token,
    factors,
    off_edge,
    blocks,
    pairs,
    rhs_edge,
    diag_edge,
    sems,
    scalar_sems,
):
    rows = rhs_h.shape[1]
    scalars = (
        pltpu.make_async_copy(blocks_h, blocks, scalar_sems.at[0]),
        pltpu.make_async_copy(pairs_h, pairs, scalar_sems.at[1]),
    )
    copies = []
    for side in range(2):
        at8, at16 = (0, 0) if side == 0 else (rows - 8, rows - 16)
        copies.append(
            (
                pltpu.make_async_copy(
                    diag_h.at[:, :, pl.ds(at8, 8)], diag_edge.at[side], sems.at[side, 0]
                ),
                pltpu.make_async_copy(
                    rhs_h.at[:, pl.ds(at8, 8)], rhs_edge.at[side], sems.at[side, 1]
                ),
                pltpu.make_async_copy(
                    off_h.at[:, :, :, pl.ds(at16, 16)], off_edge.at[side], sems.at[side, 2]
                ),
            )
        )
    for part in range(3):
        for side in range(2):
            copies[side][part].start()
    for copy in scalars:
        copy.start()
    lane = lax.broadcasted_iota(jnp.int32, (8, 128), 1)
    lus, rhss, u0s = [], [], []
    for side in range(2):
        copies[side][0].wait()
        copies[side][1].wait()
        e = lu([[diag_edge[side, a, b] for b in range(5)] for a in range(5)])
        rhs = [rhs_edge[side, a] for a in range(5)]
        u0 = solve(lambda a, b: e[a][b], rhs)
        lus.append(e)
        rhss.append(rhs)
        u0s.append(u0)
        edge_row = 0 if side == 0 else 7
        for a in range(5):
            token[pl.ds(TOKEN * side + a, 1)] = u0[a][edge_row : edge_row + 1]
            for b in range(5):
                factors[side, 5 * a + b] = e[a][b]
    for copy in scalars:
        copy.wait()
    count = blocks.shape[0]
    me = lax.axis_index("blk")
    before = lax.rem(me + count - 1, count)
    after = lax.rem(me + 1, count)
    first_end = blocks[before] != blocks[me]
    last_end = blocks[after] != blocks[me]
    codes = (
        jnp.where(first_end, jnp.maximum(pairs[0, 0], 0), 2 * before + 1),
        jnp.where(last_end, jnp.maximum(pairs[0, 1], 0), 2 * after),
    )
    for side in range(2):
        token[pl.ds(TOKEN * side + CODE_AT, 1)] = jnp.full(
            (1, 128), codes[side], jnp.int32
        ).astype(F32)
    for side in range(2):
        copies[side][2].wait()
        edge_row = 0 if side == 0 else 7
        half = slice(0, 8) if side == 0 else slice(8, 16)
        outer, inner = (0, 1) if side == 0 else (1, 0)

        def off(face, a, b):
            return off_edge[side, face, a, b].astype(F32)[half]

        e, u0 = lus[side], u0s[side]
        factor_at = lambda a, b: e[a][b]
        acc = list(rhss[side])
        for b in range(5):
            around = (
                (inner, pltpu.roll(u0[b], 7 if side == 0 else 1, 0)),
                (2, south(u0[b], lane)),
                (3, north(u0[b], lane)),
            )
            for face, value in around:
                for a in range(5):
                    acc[a] = acc[a] - off(face, a, b) * value
        base = solve(factor_at, acc)
        at = TOKEN * side
        for a in range(5):
            token[pl.ds(at + A_AT + a, 1)] = base[a][edge_row : edge_row + 1]
        for b in range(5):
            column = solve(factor_at, [off(outer, a, b) for a in range(5)])
            for a in range(5):
                token[pl.ds(at + M_AT + 5 * a + b, 1)] = column[a][edge_row : edge_row + 1]


def sweep_rows(source, rhs, off, factors, at, tile):
    lane = lax.broadcasted_iota(jnp.int32, (tile, 128), 1)
    here = pl.ds(at, tile)
    acc = [rhs[a, here] for a in range(5)]
    for b in range(5):
        middle = source[b, pl.ds(at + 8, tile)]
        around = (
            source[b, pl.ds(at + 7, tile)],
            source[b, pl.ds(at + 9, tile)],
            south(middle, lane),
            north(middle, lane),
        )
        for face in range(4):
            for a in range(5):
                acc[a] = acc[a] - off[face, a, b, here].astype(F32) * around[face]
    return solve(lambda a, b: factors[a, b, here], acc)


def early_kernel(token, rhs, off, diag, factors, first_sweep, upper, start):
    del token
    rows = rhs.shape[1]
    for b in range(5):
        for field in (start, first_sweep):
            field[b, 0:8] = jnp.zeros((8, 128), F32)
            field[b, 8 + rows : 16 + rows] = jnp.zeros((8, 128), F32)

    def factor_step(step, _):
        at = pl.multiple_of(step * FACTOR_TILE, FACTOR_TILE)
        here = pl.ds(at, FACTOR_TILE)
        e = lu([[diag[a, b, here] for b in range(5)] for a in range(5)])
        for a in range(5):
            for b in range(5):
                factors[a, b, here] = e[a][b]
        u0 = solve(lambda a, b: e[a][b], [rhs[a, here] for a in range(5)])
        for a in range(5):
            start[a, pl.ds(at + 8, FACTOR_TILE)] = u0[a]
        return 0

    def first_step(step, _):
        at = pl.multiple_of(step * TILE, TILE)
        fresh = sweep_rows(start, rhs, off, factors, at, TILE)
        for a in range(5):
            first_sweep[a, pl.ds(at + 8, TILE)] = fresh[a]
        return 0

    def second_step(step, _):
        at = pl.multiple_of(step * TILE, TILE)
        fresh = sweep_rows(first_sweep, rhs, off, factors, at, TILE)
        for a in range(5):
            upper[a, pl.ds(at, TILE)] = fresh[a]
        return 0

    lax.fori_loop(0, rows // FACTOR_TILE, factor_step, 0)
    lax.fori_loop(0, rows // TILE, first_step, 0)
    lax.fori_loop(0, upper.shape[1] // TILE, second_step, 0)


def late_kernel(rhs, off, factors, first_sweep, upper, out_h, lower, sems):
    done, left = upper.shape[1], lower.shape[1]
    copies = (
        pltpu.make_async_copy(upper, out_h.at[:, pl.ds(0, done)], sems.at[0]),
        pltpu.make_async_copy(lower, out_h.at[:, pl.ds(done, left)], sems.at[1]),
    )
    copies[0].start()

    def second_step(step, _):
        at = pl.multiple_of(step * TILE, TILE)
        fresh = sweep_rows(first_sweep, rhs, off, factors, done + at, TILE)
        for a in range(5):
            lower[a, pl.ds(at, TILE)] = fresh[a]
        return 0

    lax.fori_loop(0, left // TILE, second_step, 0)
    copies[1].start()
    for copy in copies:
        copy.wait()


def table(values, at):
    result = values[0]
    for k in range(1, len(values)):
        result = jnp.where(at == k, values[k], result)
    return result


def select_kernel(*refs):
    lines = len(refs) - PLANE - 1
    tokens, outs = refs[:lines], refs[lines + 1 :]
    me = lax.axis_index("blk")
    place = me % PLANE
    for out, step in zip(outs, (tuple(range(PLANE)),) + PLANE_STEPS):
        target = me - place + table(step, place)
        for slot in range(2):
            wanted = (2 * target + slot).astype(F32)
            found = jnp.full((TOKEN, 128), -1.0, F32)
            for token in tokens:
                for side in range(2):
                    code = token[pl.ds(TOKEN * side + CODE_AT, 1)]
                    value = token[pl.ds(TOKEN * side, TOKEN)]
                    found = jnp.where(code == wanted, value, found)
            out[pl.ds(TOKEN * slot, TOKEN)] = found


def finish_kernel(*refs):
    out_in, own, *arrived = refs[: 2 + PLANE]
    order, off_edge, factors, upper, lower, out_h, beyond, result, sems = refs[2 + PLANE :]
    rows = out_h.shape[1]
    me = lax.axis_index("blk")
    lane = lax.broadcasted_iota(jnp.int32, (8, 128), 1)
    row = lax.broadcasted_iota(jnp.int32, (8, 128), 0)
    copies = []
    for side in range(2):
        at = TOKEN * side
        half = slice(0, 8) if side == 0 else slice(8, 16)
        edge_row, next_row = (0, 1) if side == 0 else (7, 6)
        outer = outer_face(side)
        found = arrived[0][pl.ds(at, TOKEN)]
        for value in arrived[1:]:
            here = value[pl.ds(at + CODE_AT, 1)] == (2 * me + side).astype(F32)
            found = jnp.where(here, value[pl.ds(at, TOKEN)], found)
        columns = jnp.broadcast_to(order[0, side : side + 1], (8, 128))
        for first in (0, 8, 16, 24, TOKEN - 8):
            rows8 = found[first : first + 8]
            beyond[side, pl.ds(first, 8)] = jnp.take_along_axis(rows8, columns, axis=1)

        def mine(k):
            return own[pl.ds(at + k, 1)]

        def theirs(k):
            return beyond[side, pl.ds(k, 1)]

        def off(face, a, b):
            return off_edge[side, face, a, b].astype(F32)[half]

        acc = [jnp.zeros((8, 128), F32) for _ in range(5)]
        ahead, change = [], []
        for a in range(5):
            u1, delta = theirs(A_AT + a), jnp.zeros((1, 128), F32)
            for b in range(5):
                u1 = u1 - theirs(M_AT + 5 * a + b) * mine(b)
                delta = delta - mine(M_AT + 5 * a + b) * theirs(b)
            ahead.append(jnp.broadcast_to(u1, (8, 128)))
            change.append(jnp.broadcast_to(delta, (8, 128)))
        for b in range(5):
            at_edge = row == edge_row
            around = (
                (outer, jnp.where(at_edge, ahead[b], jnp.where(row == next_row, change[b], 0.0))),
                (2, jnp.where(at_edge, south(change[b], lane), 0.0)),
                (3, jnp.where(at_edge, north(change[b], lane), 0.0)),
            )
            for face, value in around:
                for a in range(5):
                    acc[a] = acc[a] + off(face, a, b) * value
        less = solve(lambda a, b: factors[side, 5 * a + b], acc)
        for a in range(5):
            near = upper[a, 0:8] if side == 0 else lower[a, pl.ds(lower.shape[1] - 8, 8)]
            result[side, a] = near - less[a]
        copies.append(
            pltpu.make_async_copy(
                result.at[side],
                out_h.at[:, pl.ds(0 if side == 0 else rows - 8, 8)],
                sems.at[side],
            )
        )
        copies[-1].start()
    for copy in copies:
        copy.wait()


def in_vmem(value):
    return pltpu.with_memory_space_constraint(value, VMEM)


def in_hbm(value):
    return pltpu.with_memory_space_constraint(value, pltpu.HBM)


def along_line(value, step, flip):
    pairs = []
    for k, to in enumerate(step):
        pairs += [(PLANE * k + j, PLANE * to + (j ^ flip)) for j in range(PLANE)]
    return lax.ppermute(value, "blk", pairs)


def within_plane(value, step):
    lines = lax.axis_size("blk") // PLANE
    pairs = [(PLANE * k + j, PLANE * k + to) for k in range(lines) for j, to in enumerate(step)]
    return lax.ppermute(value, "blk", pairs)


def on_device(right_side, off_diag, diag_block, block_of_device, interface_pairs, strip_order):
    count = lax.axis_size("blk")
    rows = right_side.shape[1]
    any_space = pl.BlockSpec(memory_space=pl.ANY)
    whole = pl.BlockSpec(memory_space=VMEM)
    token, factors_edge, off_edge = pl.pallas_call(
        edge_kernel,
        out_shape=(
            VMEM((2 * TOKEN, 128), F32),
            VMEM((2, 25, 8, 128), F32),
            VMEM((2, 4, 5, 5, 16, 128), off_diag.dtype),
        ),
        in_specs=[any_space] * 5,
        out_specs=(whole, whole, whole),
        scratch_shapes=[
            pltpu.SMEM(block_of_device.shape, jnp.int32),
            pltpu.SMEM(interface_pairs.shape, jnp.int32),
            VMEM((2, 5, 8, 128), F32),
            VMEM((2, 5, 5, 8, 128), F32),
            pltpu.SemaphoreType.DMA((2, 3)),
            pltpu.SemaphoreType.DMA((2,)),
        ],
        compiler_params=pltpu.CompilerParams(vmem_limit_bytes=8 * MIB),
        name="edges",
    )(
        in_hbm(block_of_device),
        in_hbm(interface_pairs),
        in_hbm(right_side),
        in_hbm(off_diag),
        in_hbm(diag_block),
    )

    lines = count // PLANE
    if lines <= 8:
        steps = [([k ^ by for k in range(lines)], 0) for by in range(1, lines)]
        if lines == len(LINE_STEPS[0]):
            steps = zip(LINE_STEPS, LINE_FLIPS)
        tokens = [token] + [along_line(token, step, flip) for step, flip in steps]
    else:
        groups = [[PLANE * k + j for k in range(lines)] for j in range(PLANE)]
        gathered = lax.all_gather(token, "blk", axis_index_groups=groups)
        tokens = [gathered[k] for k in range(lines)]

    rows_early = rows // 4 // TILE * TILE
    factors, first_sweep, upper = pl.pallas_call(
        early_kernel,
        out_shape=(
            VMEM((5, 5, rows, 128), F32),
            VMEM((5, rows + 16, 128), F32),
            VMEM((5, rows_early, 128), F32),
        ),
        in_specs=[any_space, whole, whole, whole],
        out_specs=(whole, whole, whole),
        scratch_shapes=[VMEM((5, rows + 16, 128), F32)],
        compiler_params=pltpu.CompilerParams(vmem_limit_bytes=12 * MIB),
        cost_estimate=pl.CostEstimate(
            flops=20000000, bytes_accessed=12 * MIB, transcendentals=0
        ),
        name="early",
    )(token, in_vmem(right_side), in_vmem(off_diag), in_vmem(diag_block))

    chosen = pl.pallas_call(
        select_kernel,
        out_shape=[VMEM((2 * TOKEN, 128), F32)] * PLANE,
        in_specs=[whole] * len(tokens) + [any_space],
        out_specs=[whole] * PLANE,
        compiler_params=pltpu.CompilerParams(vmem_limit_bytes=8 * MIB),
        name="choose",
    )(*[in_vmem(value) for value in tokens], upper)

    inside, lower = pl.pallas_call(
        late_kernel,
        out_shape=(
            pltpu.HBM(right_side.shape, F32),
            VMEM((5, rows - rows_early, 128), F32),
        ),
        in_specs=[whole] * 5,
        out_specs=(any_space, whole),
        scratch_shapes=[pltpu.SemaphoreType.DMA((2,))],
        compiler_params=pltpu.CompilerParams(vmem_limit_bytes=8 * MIB),
        cost_estimate=pl.CostEstimate(
            flops=8000000, bytes_accessed=6 * MIB, transcendentals=0
        ),
        name="late",
    )(*[in_vmem(value) for value in (right_side, off_diag, factors, first_sweep, upper)])
    arrived = [chosen[0]]
    for value, step in zip(chosen[1:], PLANE_STEPS):
        arrived.append(within_plane(value, step))

    return pl.pallas_call(
        finish_kernel,
        out_shape=pltpu.HBM(right_side.shape, F32),
        in_specs=[any_space] + [whole] * (1 + PLANE + 5),
        out_specs=any_space,
        scratch_shapes=[
            VMEM((2, TOKEN + 4, 128), F32),
            VMEM((2, 5, 8, 128), F32),
            pltpu.SemaphoreType.DMA((2,)),
        ],
        input_output_aliases={0: 0},
        compiler_params=pltpu.CompilerParams(vmem_limit_bytes=8 * MIB),
        name="finish",
    )(
        in_hbm(inside),
        in_vmem(token),
        *[in_vmem(value) for value in arrived],
        strip_order,
        in_vmem(off_edge),
        in_vmem(factors_edge),
        in_vmem(upper),
        in_vmem(lower),
    )


def solution(mesh):
    return jax.shard_map(
        on_device,
        mesh=mesh,
        in_specs=(
            P(None, ("parts", "blk"), None),
            P(None, None, None, ("parts", "blk"), None),
            P(None, None, ("parts", "blk"), None),
            P(),
            P("blk", None),
            P("blk", None, None),
        ),
        out_specs=P(None, ("parts", "blk"), None),
        check_vma=False,
    )
```
